256 devices in a mesh: group: 8 (over y, core), sub: 32 (over z, x).
Axes of the slice: x: 4, y: 4, z: 8, core: 2. Of those that a mesh axis runs over, the one named last changes fastest.
Arguments:
- residual_in: float32 [128, 9, 32768], P(None, None, ('group', 'sub')), may hold values from -64 to 64
- local_inverse: bfloat16 [256, 2304, 2304], P(('group', 'sub')), may hold values from -0.5 to 1.75
- coarse_inverse: bfloat16 [11520, 11520], P(('group', 'sub')), may hold values from -1 to 1
- cluster_of: int32 [32768], P(('group', 'sub')), may hold values from 0 to 159
- margin_peer: int32 [32768, 1], P(('group', 'sub')), may hold values from 0 to 31; in each aligned block of 128 rows (0 to 127, 128 to 255, ...) at most 8 rows name the same one
- margin_row: int32 [32768], P(('group', 'sub')), may hold values from 0 to 127
Outputs:
- first: float32 [128, 9, 32768], P(None, None, ('group', 'sub'))
- second: float32 [128, 9, 32768], P(None, None, ('group', 'sub'))
The draws below stay inside these ranges and needn't reach their ends.
Inputs may be any that keep to these rules, and one draw needn't show every extreme that they name: `margin_peer`: among the 128 margin slots of one subdomain no sub index appears more than 8 times, and some subdomain names one exactly 8 times.
All inputs are finite; a program needn't handle non-finite values.
Results may differ from the reference program's by a relative error of at most 0.015.
Values may be sent and summed in bfloat16 or wider, within the bound.
No kernel may reach another device: no remote copies, remote signals or barrier semaphores. Data moves between devices by JAX's collectives and lax.ppermute only.
A program may use at most 128 MiB of HBM per device.

```python
import math
import jax
import jax.numpy as jnp
import numpy as np
from jax import lax

NRHS = 128
COMP = 9
SUB_CAM = 256
OWN_CAM = 128
CL_DEV = 5
SUB = 2304
OVL_CAM = 128
CAP = 8
SUBS = 256
CAMS = 32768
CL_GRP = 160
CLUSTERS = 1280
CO = 11520
N_SUB = 32


def draw_residual_in(key, part):
    key = jax.random.fold_in(key, 11)
    key_base, key_cam, key_rhs = jax.random.split(key, 3)
    cameras = jnp.arange(CAMS)
    position = (cameras // OWN_CAM).astype(jnp.float32) / max(SUBS - 1, 1)
    ramp = jnp.exp(position * math.log(3.0)) / 1.7320508
    cam_scale = jnp.exp(jax.random.uniform(key_cam, (CAMS,), jnp.float32, math.log(0.3), math.log(3.0)))
    rhs_scale = jnp.exp(jax.random.uniform(key_rhs, (NRHS, 1, 1), jnp.float32, math.log(0.3), math.log(3.0)))
    base = jnp.clip(jax.random.normal(key_base, (NRHS, COMP, CAMS), jnp.float32), -4.0, 4.0)
    return (base * (cam_scale * ramp)[None, None, :] * rhs_scale).astype(jnp.float32)


def draw_local_inverse(key, part):
    key = jax.random.fold_in(key, 12)
    key_off = jax.random.fold_in(key, 0)
    row_index = lax.broadcasted_iota(jnp.int32, (1, SUB, SUB), 1)
    col_index = lax.broadcasted_iota(jnp.int32, (1, SUB, SUB), 2)
    identity = (row_index == col_index).astype(jnp.float32)
    spread_off = 0.6 / math.sqrt(SUB)
    off_part = jnp.clip(jax.random.normal(key_off, (SUBS, SUB, SUB), jnp.float32), -4.0, 4.0) * spread_off
    diag_part = jnp.ones((SUBS, SUB, 1), jnp.float32)
    return (identity * diag_part + off_part).astype(jnp.bfloat16)


def draw_coarse_inverse(key, part):
    key = jax.random.fold_in(key, 13)
    key_off = jax.random.fold_in(key, 0)
    key_far = jax.random.fold_in(key, 2)
    row_index = lax.broadcasted_iota(jnp.int32, (CO, CO), 0)
    col_index = lax.broadcasted_iota(jnp.int32, (CO, CO), 1)
    identity = (row_index == col_index).astype(jnp.float32)
    block_rows = CL_DEV * COMP
    row_owner = row_index // block_rows
    col_owner = col_index // block_rows
    far_mask = (col_owner == (row_owner + SUBS // 2) % SUBS).astype(jnp.float32)
    diag_value = 2.0 * CL_DEV / OWN_CAM
    spread_off = 0.5 * diag_value / math.sqrt(CO)
    spread_far = 0.8 * diag_value / math.sqrt(block_rows)
    off_part = jnp.clip(jax.random.normal(key_off, (CO, CO), jnp.float32), -4.0, 4.0) * spread_off
    far_part = jnp.clip(jax.random.normal(key_far, (CO, CO), jnp.float32), -4.0, 4.0) * spread_far
    diag_part = diag_value * jnp.ones((CO, 1), jnp.float32)
    return (identity * diag_part + off_part + far_mask * far_part).astype(jnp.bfloat16)


def place_ends(result, key, smallest, largest):
    dims = result.shape
    place = [jax.random.randint(jax.random.fold_in(key, axis), (), 0, dims[axis]) for axis in range(len(dims))]
    result = result.at[tuple(place)].set(smallest)
    longest = dims.index(max(dims))
    place[longest] = (place[longest] + 1) % dims[longest]
    return result.at[tuple(place)].set(largest)


def assign_block(stream_key, own, number, rows, amount, top, most, lean):
    sequence = jax.random.permutation(stream_key, amount)
    heavy_load, usual = portions_of(amount, rows * top, most, lean, True), portions_of(amount, rows * top, most, lean, False)
    places = jnp.arange(amount)

    def named(lengths, offset_by):
        used = int((lengths > 0).sum())
        fixed = max(1, used // 4)
        passed = fixed + (places - fixed + offset_by * (used - fixed)) % max(1, amount - fixed)
        return jnp.zeros((amount,), jnp.int32).at[sequence[jnp.where(places < fixed, places, passed)]].set(jnp.asarray(lengths, jnp.int32))

    lengths = jnp.where(number % 4 == 0, named(heavy_load, number // 4), named(usual, number - number // 4 - 1))
    mixed = jax.random.permutation(jax.random.fold_in(own, 3), amount)
    source_of, taker = mixed[0:amount // 2 * 2:2], mixed[1:amount // 2 * 2:2]
    room = jnp.minimum(lengths[source_of] - 1, most - lengths[taker]) // 2
    room = jnp.where((source_of == sequence[0]) | (taker == sequence[0]) | (lengths[taker] == 0), 0, jnp.maximum(room, 0))
    passed = jax.random.randint(jax.random.fold_in(own, 4), (amount // 2,), 0, 1 << 20) % (room + 1)
    lengths = lengths.at[source_of].add(-passed).at[taker].add(passed)
    items = jnp.searchsorted(jnp.cumsum(lengths), jnp.arange(rows * top), side="right").astype(jnp.int32)
    grid = items.reshape(top, rows).T
    grid = grid[jax.random.permutation(jax.random.fold_in(own, 1), rows)]
    offset_by = jax.random.randint(jax.random.fold_in(own, 2), (rows, 1), 0, top)
    return jnp.take_along_axis(grid, (jnp.arange(top)[None, :] + offset_by) % top, axis=1)


def portions_of(number_of, total, bound, skew, full):
    weights = [(1 << 20) // math.isqrt(standing ** skew) + 1 for standing in range(1, number_of + 1)]
    largest = bound if full else min(bound, max(-(-total // number_of), total * weights[0] // sum(weights)))
    least = 1 if total - largest >= number_of - 1 else 0
    given, spare = [largest] + [least] * (number_of - 1), total - largest - least * (number_of - 1)
    while spare > 0:
        free = [i for i in range(1, number_of) if given[i] < largest] or [i for i in range(1, number_of) if given[i] < bound]
        mass, budget = sum([weights[i] for i in free]), spare
        for i in free:
            addition = min(bound - given[i], max(1, budget * weights[i] // mass), spare)
            given[i] = given[i] + addition
            spare = spare - addition
    return np.array(given)


def setup_inputs(seed: int = 0) -> dict:
    streams_of = jax.random.split(jax.random.key(seed), 7)
    residual_in = draw_residual_in(jax.random.fold_in(streams_of[6], 71), 0)
    local_inverse = draw_local_inverse(jax.random.fold_in(streams_of[6], 71), 0)
    coarse_inverse = draw_coarse_inverse(jax.random.fold_in(streams_of[6], 71), 0)
    cluster_of = place_ends(jax.random.randint(streams_of[3], (CAMS,), 0, CL_GRP), jax.random.fold_in(streams_of[3], 1), 0, CL_GRP - 1).astype(jnp.int32)
    margin_peer_keys = jax.random.split(jax.random.fold_in(streams_of[4], 1), (SUBS * OVL_CAM) // OVL_CAM)
    margin_peer_turns = jax.random.permutation(jax.random.fold_in(streams_of[4], 3), (SUBS * OVL_CAM) // OVL_CAM)
    margin_peer = jax.vmap(lambda own, number: assign_block(jax.random.fold_in(streams_of[4], 2), own, number, OVL_CAM, N_SUB, 1, CAP, 2))(margin_peer_keys, margin_peer_turns).reshape((SUBS * OVL_CAM, 1))
    margin_row = place_ends(jax.random.randint(streams_of[5], (SUBS * OVL_CAM,), 0, OWN_CAM), jax.random.fold_in(streams_of[5], 1), 0, OWN_CAM - 1).astype(jnp.int32)
    return {"residual_in": residual_in, "local_inverse": local_inverse, "coarse_inverse": coarse_inverse, "cluster_of": cluster_of, "margin_peer": margin_peer, "margin_row": margin_row}


EPSILON = 1e-6


def subdomain_part(source, local_inverse, camera_ids):
    own_part = source.reshape(NRHS, COMP, SUBS, OWN_CAM)
    over_part = jnp.take(source, camera_ids, axis=2)
    joined = jnp.concatenate([own_part, over_part], axis=3).astype(jnp.bfloat16)
    joined = jnp.transpose(joined, (2, 0, 1, 3)).reshape(SUBS, NRHS, SUB)

    def solve_one(paired):
        block_in, inverse = paired
        return jnp.dot(block_in, inverse, preferred_element_type=jnp.float32)

    local_out = lax.map(solve_one, (joined, local_inverse))
    local_out = jnp.transpose(local_out.reshape(SUBS, NRHS, COMP, SUB_CAM), (1, 2, 0, 3))
    spread = local_out[:, :, :, :OWN_CAM].reshape(NRHS, COMP, CAMS)
    over_out = local_out[:, :, :, OWN_CAM:].reshape(NRHS, COMP, SUBS * OVL_CAM)
    return spread.at[:, :, camera_ids.reshape(-1)].add(over_out)


def coarse_part(source, coarse_inverse, cluster_ids):
    sums = jax.ops.segment_sum(jnp.transpose(source, (2, 0, 1)), cluster_ids, num_segments=CLUSTERS)
    coarse_in = jnp.transpose(sums, (1, 0, 2)).reshape(NRHS, CO).astype(jnp.bfloat16)
    coarse_sol = lax.dot_general(coarse_in, coarse_inverse, (((1,), (1,)), ((), ())), preferred_element_type=jnp.float32)
    coarse_sol = coarse_sol.reshape(NRHS, CLUSTERS, COMP)
    return jnp.transpose(jnp.take(coarse_sol, cluster_ids, axis=1), (0, 2, 1))


def precondition(source, local_inverse, coarse_inverse, camera_ids, cluster_ids):
    return subdomain_part(source, local_inverse, camera_ids) + coarse_part(source, coarse_inverse, cluster_ids)


def reference(residual_in, local_inverse, coarse_inverse, cluster_of, margin_peer, margin_row):
    peer_ids = margin_peer[:, 0].reshape(SUBS, OVL_CAM)
    row_ids = margin_row.reshape(SUBS, OVL_CAM)
    group_base = (jnp.arange(SUBS, dtype=jnp.int32) // N_SUB) * N_SUB
    camera_ids = ((group_base[:, None] + peer_ids) * OWN_CAM + row_ids).astype(jnp.int32)
    cameras = jnp.arange(CAMS, dtype=jnp.int32)
    cluster_ids = ((cameras // (OWN_CAM * N_SUB)) * CL_GRP + cluster_of).astype(jnp.int32)
    first = precondition(residual_in, local_inverse, coarse_inverse, camera_ids, cluster_ids)
    inner_rf = jnp.sum(residual_in * first, axis=(1, 2))
    inner_ff = jnp.sum(first * first, axis=(1, 2))
    step_scale = inner_rf / (inner_ff + EPSILON)
    shifted = residual_in - step_scale[:, None, None] * first
    second = precondition(shifted, local_inverse, coarse_inverse, camera_ids, cluster_ids)
    return first, second
```

```python
import jax
import jax.numpy as jnp
from jax import lax
from jax.sharding import PartitionSpec as P

EPSILON = 1e-06
F32 = jnp.float32
BF16 = jnp.bfloat16


def dot(left, right):
    return jnp.dot(left, right, preferred_element_type=F32)


def hot(ids, count):
    return (ids[:, None] == jnp.arange(count, dtype=jnp.int32)[None, :]).astype(BF16)


def hot_t(ids, count):
    return (jnp.arange(count, dtype=jnp.int32)[:, None] == ids[None, :]).astype(BF16)


def exchange(values, axis):
    return lax.all_to_all(values, axis, split_axis=0, concat_axis=0, tiled=True)


def body(residual_in, local_inverse, coarse_inverse, cluster_of, margin_peer, margin_row):
    rhs, comps, own = residual_in.shape
    over = margin_row.shape[0]
    subs = lax.axis_size("sub")
    groups = lax.axis_size("group")
    cap = max(2, 2 * over // subs)
    slots = subs * cap
    cl_rows = coarse_inverse.shape[0]
    cl_dev = cl_rows // comps
    cl_grp = cl_dev * subs
    grp_rows = cl_rows * subs
    width = local_inverse.shape[1]
    cams = width // comps
    lanes = comps * rhs
    inverse = local_inverse[0]

    def aux_row(values):
        return jnp.pad(values, ((0, 0), (0, lanes - values.shape[1])))[:, None, :].astype(BF16)

    def spread_out(values):
        return jnp.broadcast_to(values.astype(BF16)[None], (subs,) + values.shape)

    with jax.named_scope("coarse_block"):
        columns = coarse_inverse.reshape(cl_rows, groups, grp_rows).transpose(1, 0, 2)
        coarse_block = exchange(columns, "group").reshape(groups * cl_rows, grp_rows)

    with jax.named_scope("index"):
        peer = margin_peer[:, 0]
        place = jnp.arange(over, dtype=jnp.int32)
        earlier = (peer[:, None] == peer[None, :]) & (place[None, :] < place[:, None])
        dest = peer * cap + jnp.sum(earlier.astype(jnp.int32), axis=1)
        take = hot(dest, slots)
        take_t = hot_t(dest, slots)
        wanted = jnp.sum(
            jnp.where(jnp.arange(slots, dtype=jnp.int32)[:, None] == dest[None, :], margin_row[None, :] + 1, 0),
            axis=1,
        )
        own_hot = hot_t(cluster_of, cl_grp)
        own_back = hot(cluster_of, cl_grp)
        counts = jnp.sum(own_hot.astype(F32), axis=1)

    with jax.named_scope("restrict"):
        field = residual_in.transpose(2, 1, 0).reshape(own, lanes)
        field16 = field.astype(BF16)
        sums = dot(own_hot, field16).astype(BF16).reshape(subs, cl_dev, lanes)
        extra = aux_row(
            jnp.concatenate([wanted.reshape(subs, cap).astype(F32), counts.reshape(subs, cl_dev)], axis=1)
        )
        got = exchange(jnp.concatenate([sums, extra], axis=1), "sub")
        coarse_in = jnp.sum(got[:, :cl_dev].astype(F32), axis=0)
        asked = got[:, cl_dev, :cap].astype(jnp.int32).reshape(slots) - 1
        members = jnp.sum(got[:, cl_dev, cap : cap + cl_dev].astype(F32), axis=0)[:, None]
        give = hot(asked, own)
        give_t = hot_t(asked, own)

    def solve(own_part, over_part):
        joined = jnp.concatenate([own_part, over_part], axis=0).reshape(cams, comps, rhs)
        flat = joined.transpose(1, 0, 2).reshape(width, rhs)
        result = lax.dot_general(flat, inverse, (((0,), (0,)), ((), ())), preferred_element_type=F32)
        return result.reshape(rhs, comps, cams).transpose(2, 1, 0).reshape(cams, lanes)

    def coarse(gathered, inner):
        column = gathered.reshape(grp_rows, rhs)
        parts = dot(coarse_block, column).reshape(groups, cl_rows, rhs)
        if inner is not None:
            parts = jnp.concatenate([parts, jnp.broadcast_to(inner[None], (groups,) + inner.shape)], axis=1)
        total = jnp.sum(exchange(parts, "group"), axis=0)
        return total[:cl_rows].reshape(cl_dev, lanes), total[cl_rows:]

    with jax.named_scope("fetch_first"):
        clusters = jnp.sum(
            jnp.where(asked[:, None] == jnp.arange(own, dtype=jnp.int32)[None, :], cluster_of[None, :], 0), axis=1
        ).astype(F32)
        sent = jnp.concatenate(
            [
                dot(give, field16).astype(BF16).reshape(subs, cap, lanes),
                spread_out(coarse_in),
                aux_row(clusters.reshape(subs, cap)),
            ],
            axis=1,
        )
        got = exchange(sent, "sub")
        over_field = dot(take, got[:, :cap].reshape(slots, lanes)).astype(BF16)
        over_ids = dot(take, got[:, cap + cl_dev, :cap].reshape(slots, 1))[:, 0].astype(jnp.int32)
        over_hot = hot_t(over_ids, cl_grp)
        over_back = hot(over_ids, cl_grp)
    with jax.named_scope("coarse_first"):
        sol, _ = coarse(got[:, cap : cap + cl_dev].reshape(cl_grp, lanes), None)
    with jax.named_scope("solve_first"):
        result = solve(field16, over_field)
        result16 = result.astype(BF16)

    with jax.named_scope("return_first"):
        sums = dot(jnp.concatenate([own_hot, over_hot], axis=1), result16).astype(BF16)
        back = dot(take_t, result16[own:]).astype(BF16)
        sent = jnp.concatenate([back.reshape(subs, cap, lanes), sums.reshape(subs, cl_dev, lanes)], axis=1)
        got = exchange(sent, "sub")
        spread = result[:own] + dot(give_t, got[:, :cap].reshape(slots, lanes))
        coarse_in = jnp.sum(got[:, cap:].astype(F32), axis=0) + members * sol

    with jax.named_scope("fetch_second"):
        sent = jnp.concatenate(
            [
                dot(give, spread.astype(BF16)).astype(BF16).reshape(subs, cap, lanes),
                spread_out(coarse_in),
                spread_out(sol),
            ],
            axis=1,
        )
        got = exchange(sent, "sub")
        solution_all = got[:, cap + cl_dev :].reshape(cl_grp, lanes)
        first = spread + dot(own_back, solution_all)
        over_first = dot(take, got[:, :cap].reshape(slots, lanes)) + dot(over_back, solution_all)
        inner = jnp.stack(
            [
                jnp.sum((field * first).reshape(own * comps, rhs), axis=0),
                jnp.sum((first * first).reshape(own * comps, rhs), axis=0),
            ]
        )
    with jax.named_scope("coarse_second"):
        sol, inner = coarse(got[:, cap : cap + cl_dev].reshape(cl_grp, lanes), inner)
    with jax.named_scope("solve_second"):
        result = solve(first.astype(BF16), over_first.astype(BF16))

    with jax.named_scope("return_second"):
        back = dot(take_t, result[own:].astype(BF16)).astype(BF16)
        high = inner.astype(BF16)
        low = inner - high.astype(F32)
        pair = jnp.concatenate([high.astype(F32), low], axis=0).reshape(1, 4 * rhs)
        sent = jnp.concatenate(
            [
                back.reshape(subs, cap, lanes),
                spread_out(sol),
                aux_row(jnp.broadcast_to(pair, (subs, 4 * rhs))),
            ],
            axis=1,
        )
        got = exchange(sent, "sub")
        solution_all = got[:, cap : cap + cl_dev].reshape(cl_grp, lanes)
        applied = result[:own] + dot(give_t, got[:, :cap].reshape(slots, lanes)) + dot(own_back, solution_all)
        pair = jnp.sum(got[:, cap + cl_dev, : 4 * rhs].astype(F32), axis=0).reshape(2, 2, rhs)
        inner = pair[0] + pair[1]
        scale = inner[0] / (inner[1] + EPSILON)
        second = first - jnp.tile(scale, comps)[None, :] * applied

    def place_out(values):
        return values.reshape(own, comps, rhs).transpose(2, 1, 0)

    return place_out(first), place_out(second)


def solution(mesh):
    placed = (
        P(None, None, ("group", "sub")),
        P(("group", "sub"), None, None),
        P(("group", "sub"), None),
        P(("group", "sub")),
        P(("group", "sub"), None),
        P(("group", "sub")),
    )
    return jax.shard_map(
        body,
        mesh=mesh,
        in_specs=placed,
        out_specs=(P(None, None, ("group", "sub")), P(None, None, ("group", "sub"))),
        check_vma=False,
    )
```

```python
import functools

import jax
import jax.numpy as jnp
import numpy as np
from jax import lax
from jax.experimental import pallas as pl
from jax.experimental.pallas import tpu as pltpu
from jax.sharding import PartitionSpec as P

EPSILON = 1e-06
F32 = jnp.float32
BF16 = jnp.bfloat16
LANES = 128
ROWS = 8


def dot(left, right):
    return jnp.dot(left, right, preferred_element_type=F32)


def exchange(values, axis):
    return lax.all_to_all(values, axis, split_axis=0, concat_axis=0, tiled=True)


def tile(values, index):
    return values[:, index * LANES : (index + 1) * LANES]


def iota(shape, axis):
    return lax.broadcasted_iota(jnp.int32, shape, axis)


def over_rows(values, subs):
    cube = values.reshape(subs, ROWS, LANES)
    return jnp.broadcast_to(jnp.sum(cube, axis=1, keepdims=True), cube.shape).reshape(subs * ROWS, LANES)


def one_row(values, row, subs):
    cube = values.reshape(subs, ROWS, LANES)
    return jnp.broadcast_to(cube[:, row : row + 1, :], cube.shape).reshape(subs * ROWS, LANES)


def repeat_rows(values, subs):
    return jnp.broadcast_to(values[None], (subs,) + values.shape).reshape(subs * ROWS, values.shape[1])


def kernel_call(body, outs, *args, **kw):
    return pl.pallas_call(
        body,
        out_shape=[jax.ShapeDtypeStruct(shape, dtype) for shape, dtype in outs],
        compiler_params=pltpu.CompilerParams(vmem_limit_bytes=48 * 1024 * 1024),
        **kw,
    )(*args)


def make(rhs, comps, own, over, subs, groups, cl_dev):
    tail = ROWS - cl_dev
    main = comps - tail
    slots = subs * ROWS
    lanes = comps * LANES
    block = main * LANES
    aux = main - 1

    def pack(sums, extra, ref, offset):
        inner = iota((slots, LANES), 0) % ROWS
        for t in range(main):
            value = tile(sums, t)
            if t < cl_dev:
                for j in range(tail):
                    value = jnp.where(inner == cl_dev + j, one_row(tile(sums, main + j), t, subs), value)
            elif extra is not None:
                value = jnp.where(inner == cl_dev, extra, value)
            ref[:, offset + t * LANES : offset + (t + 1) * LANES] = value.astype(BF16)

    def prolong(tiles, own8t, own_tail, own_kind):
        head = dot(own8t, tiles)
        picked = dot(own_tail, tiles[:, : cl_dev * LANES])
        parts = [head]
        for j in range(tail):
            rows = picked[j * own : (j + 1) * own]
            value = jnp.zeros((own, LANES), F32)
            for t in range(cl_dev):
                value = jnp.where(own_kind == t, tile(rows, t), value)
            parts.append(value)
        return jnp.concatenate(parts, axis=1)

    def begin(res, cl, peer, row, field, field16, fieldr, send, own8, own8t, own_tail, own_kind, take, take_t):
        for k in range(comps):
            values = res[:, k, :]
            turned = values.T
            field[:, k * LANES : (k + 1) * LANES] = turned
            field16[:, k * LANES : (k + 1) * LANES] = turned.astype(BF16)
            fieldr[:, k * LANES : (k + 1) * LANES] = values.astype(BF16)
        number = cl[...]
        holder = ((number.astype(F32) + 0.5) * (1.0 / cl_dev)).astype(jnp.int32)
        kind = number - holder * cl_dev
        rows = iota((slots, own), 0)
        lane = iota((slots, LANES), 1)
        inner = rows % ROWS
        hot = (rows == holder * ROWS + kind).astype(F32)
        own8[...] = hot.astype(BF16)
        own8t[...] = hot.T.astype(BF16)
        for j in range(tail):
            hot_j = (rows == holder * ROWS + (cl_dev + j)).astype(F32)
            own_tail[j * own : (j + 1) * own, :] = hot_j.T.astype(BF16)
        own_kind[...] = jnp.broadcast_to(kind.astype(F32), (LANES, own)).T
        peers = jnp.broadcast_to(peer[...].astype(F32), (over, over))
        same = (peers == peers.T) & (iota((over, over), 0) < iota((over, over), 1))
        rank = jnp.sum(same.astype(F32), axis=0, keepdims=True).astype(jnp.int32)
        dest = peer[...] * ROWS + rank
        hot_dest = (iota((slots, over), 0) == dest).astype(F32)
        take_t[...] = hot_dest.astype(BF16)
        take[...] = hot_dest.T.astype(BF16)
        wanted = jnp.sum(hot_dest * (row[...] + 1).astype(F32), axis=1, keepdims=True)
        counts = jnp.sum(hot, axis=1, keepdims=True)
        extra = jnp.where(lane == inner, wanted, 0.0) + jnp.where(lane == inner + ROWS, counts, 0.0)
        pack(dot(own8[...], field16[...]), over_rows(extra, subs), send, 0)

    def answer(got, field16, cl, send, give, give_t, members):
        lane = iota((slots, LANES), 1)
        inner = iota((slots, LANES), 0) % ROWS
        total = jnp.sum(got[...].astype(F32).reshape(subs, ROWS, block), axis=0)
        asked = one_row(tile(got, aux).astype(F32), cl_dev, subs)
        asked = jnp.sum(jnp.where(lane == inner, asked, 0.0), axis=1, keepdims=True) - 1.0
        hot = (iota((slots, own), 1).astype(F32) == asked).astype(F32)
        give[...] = hot.astype(BF16)
        give_t[...] = hot.T.astype(BF16)
        send[:, :lanes] = dot(give[...], field16[...]).astype(BF16)
        ids = jnp.sum(hot * cl[...].astype(F32), axis=1, keepdims=True)
        ids = over_rows(jnp.where(lane == inner, ids, 0.0), subs)
        small = iota((ROWS, LANES), 0)
        small_lane = iota((ROWS, LANES), 1)
        numbers = [
            jnp.sum(
                jnp.where((small_lane == ROWS + c) & (small == cl_dev), tile(total, aux), 0.0),
                axis=(0, 1),
                keepdims=True,
            )
            for c in range(cl_dev)
        ]
        base = jnp.zeros((ROWS, LANES), F32)
        for c in range(cl_dev):
            base = jnp.where(small == c, numbers[c], base)
        for t in range(main):
            value = repeat_rows(tile(total, t), subs)
            count = base
            if t < cl_dev:
                count = jnp.where(small < cl_dev, base, numbers[t])
            else:
                value = jnp.where(inner == cl_dev, ids, value)
            send[:, lanes + t * LANES : lanes + (t + 1) * LANES] = value.astype(BF16)
            members[:, t * LANES : (t + 1) * LANES] = count

    def coarse(offset, rows, matrix, got, *refs):
        out = refs[-1]
        total = jnp.zeros((matrix.shape[0], LANES), F32)
        for t in range(main):
            total += dot(matrix[:, t * slots : (t + 1) * slots], got[:, offset + t * LANES : offset + (t + 1) * LANES])
        each = main * ROWS
        for g in range(groups):
            out[g, :each, :] = total[g * each : (g + 1) * each].astype(BF16)
        if rows > each:
            inner = refs[0][...]
            high = inner.astype(BF16).astype(F32)
            last = jnp.concatenate([high, inner - high, jnp.zeros((rows - each - 4, LANES), F32)], axis=0)
            for g in range(groups):
                out[g, each:, :] = last.astype(BF16)

    def group_total(got):
        total = jnp.sum(got[...].astype(F32), axis=0)
        return total, [total[t * ROWS : (t + 1) * ROWS] for t in range(main)]

    def half(fieldr, inverse, out):
        step = pl.program_id(0)
        columns = pl.ds(pl.multiple_of(step * fieldr.shape[1] // 3, LANES), fieldr.shape[1] // 3)
        product = dot(fieldr[:, columns], inverse[...].reshape(fieldr.shape[1] // 3, inverse.shape[-1]))

        @pl.when(step == 0)
        def _():
            out[...] = product

        @pl.when(step > 0)
        def _():
            out[...] += product

    def half_first(values, field, inverse, first_out, inner, out, turned):
        @pl.when(pl.program_id(0) == 0)
        def _():
            rf = jnp.zeros((1, LANES), F32)
            ff = jnp.zeros((1, LANES), F32)
            for k in range(comps):
                mine = tile(values, k)
                flipped = mine.T
                first_out[:, k, :] = flipped
                turned[:, k * LANES : (k + 1) * LANES] = flipped.astype(BF16)
                rf += jnp.sum(tile(field, k) * mine, axis=0, keepdims=True)
                ff += jnp.sum(mine * mine, axis=0, keepdims=True)
            inner[...] = jnp.concatenate([rf, ff], axis=0)

        half(turned, inverse, out)

    def finish(full, got, part, inverse, take, take_t, own8, res_own, send, turned, total, own16, over16):
        step = pl.program_id(0)

        @pl.when(step == 0)
        def _():
            arrived = dot(take[...], got[:, :lanes])
            for k in range(comps):
                turned[:, k * LANES : (k + 1) * LANES] = tile(arrived, k).T.astype(BF16)
            total[...] = part[...]

        third = lanes // 3
        columns = pl.ds(pl.multiple_of(step * third, LANES), third)
        total[...] += dot(turned[:, columns], inverse[...].reshape(third, inverse.shape[-1]))

        @pl.when(step == 2)
        def _():
            cams = own + over
            for k in range(comps):
                flipped = total[:, k * cams : (k + 1) * cams].T
                res_own[:, k * LANES : (k + 1) * LANES] = flipped[:own]
                if full:
                    own16[:, k * LANES : (k + 1) * LANES] = flipped[:own].astype(BF16)
                over16[:, k * LANES : (k + 1) * LANES] = flipped[own:].astype(BF16)
            send[:, :lanes] = dot(take_t[...], over16[...]).astype(BF16)
            if full:
                lane = iota((slots, LANES), 1)
                inner = iota((slots, LANES), 0) % ROWS
                ids = one_row(got[:, lanes + aux * LANES : lanes + (aux + 1) * LANES].astype(F32), cl_dev, subs)
                ids = jnp.sum(jnp.where(lane == inner, ids, 0.0), axis=1, keepdims=True)
                number = jnp.sum(take_t[...].astype(F32) * ids, axis=0, keepdims=True)
                holder = ((number + 0.5) * (1.0 / cl_dev)).astype(jnp.int32)
                kind = number.astype(jnp.int32) - holder * cl_dev
                over8 = (iota((slots, over), 0) == holder * ROWS + kind).astype(F32).astype(BF16)
                sums = dot(own8[...], own16[...]) + dot(over8, over16[...])
                pack(sums, None, send, lanes)

    def join_first(sent, got, send, sol):
        send[:, : lanes + block] = sent[...]
        _, tiles = group_total(got)
        for t in range(main):
            sol[:, t * LANES : (t + 1) * LANES] = tiles[t]
            send[:, lanes + block + t * LANES : lanes + block + (t + 1) * LANES] = repeat_rows(tiles[t], subs).astype(BF16)

    def join_second(sent, got, send):
        send[:, :lanes] = sent[...]
        total, tiles = group_total(got)
        each = main * ROWS
        inner = total[each : each + 2] + total[each + 2 : each + 4]
        small = iota((ROWS, LANES), 0)
        for t in range(main):
            value = tiles[t]
            if t == aux:
                value = jnp.where(small == cl_dev, inner[0:1], value)
                value = jnp.where(small == cl_dev + 1, inner[1:2], value)
            send[:, lanes + t * LANES : lanes + (t + 1) * LANES] = repeat_rows(value, subs).astype(BF16)

    def combine(got, res_own, give, give_t, own8t, own_tail, own_kind, members, sol, first, send):
        values = res_own[...] + dot(give_t[...], got[:, :lanes])
        values += prolong(got[:, lanes + block :], own8t[...], own_tail[...], own_kind[...])
        first[...] = values
        send[:, :lanes] = dot(give[...], values.astype(BF16)).astype(BF16)
        total = jnp.sum(got[:, lanes : lanes + block].astype(F32).reshape(subs, ROWS, block), axis=0)
        total += members[...] * sol[...]
        send[:, lanes:] = repeat_rows(total, subs).astype(BF16)

    def end(got, res_own, first, give_t, own8t, own_tail, own_kind, out):
        applied = res_own[...] + dot(give_t[...], got[:, :lanes])
        applied += prolong(got[:, lanes:], own8t[...], own_tail[...], own_kind[...])
        sums = got[:, lanes + aux * LANES :].astype(F32).reshape(subs, ROWS, LANES)
        sums = jnp.sum(sums, axis=0)
        scale = sums[cl_dev : cl_dev + 1] / (sums[cl_dev + 1 : cl_dev + 2] + EPSILON)
        for k in range(comps):
            out[:, k, :] = (tile(first, k) - scale * tile(applied, k)).T

    return dict(locals())


def block_order(cl_dev, comps, count):
    tail = ROWS - cl_dev
    main = comps - tail
    order = np.full((main, count, ROWS), -1, np.int32)
    for t in range(main):
        for i in range(ROWS):
            if i < cl_dev:
                order[t, :, i] = np.arange(count) * cl_dev * comps + i * comps + t
            elif t < cl_dev:
                order[t, :, i] = np.arange(count) * cl_dev * comps + t * comps + main + i - cl_dev
    return order.reshape(-1)


def regroup(coarse_inverse, groups, subs, cl_dev, comps):
    cl_rows = cl_dev * comps
    grp_rows = cl_rows * subs
    row_order = block_order(cl_dev, comps, 1)
    col_order = block_order(cl_dev, comps, subs)
    pick_rows = jnp.asarray(row_order[:, None] == np.arange(cl_rows)[None, :]).astype(BF16)
    pick_cols = (jnp.asarray(col_order)[None, :] == jnp.arange(grp_rows, dtype=jnp.int32)[:, None]).astype(BF16)
    values = coarse_inverse.reshape(cl_rows, groups, grp_rows)
    values = lax.dot_general(pick_rows, values, (((1,), (0,)), ((), ())), preferred_element_type=F32).astype(BF16)
    values = values.transpose(1, 0, 2).reshape(groups * row_order.size, grp_rows)
    values = dot(values, pick_cols).astype(BF16).reshape(groups, row_order.size, col_order.size)
    if groups == 1:
        return values.reshape(-1, col_order.size)
    turns = groups // 2
    index = lax.axis_index("group")
    core, turn = index % 2, index // 2
    pairs = values.reshape(turns, 2, row_order.size, col_order.size)
    kept = lax.dynamic_index_in_dim(pairs, core, 1, keepdims=False)
    given = lax.dynamic_index_in_dim(pairs, 1 - core, 1, keepdims=False)
    other = lax.ppermute(given, "group", [(i, i ^ 1) for i in range(groups)])
    both = jnp.where(core == 0, jnp.stack([kept, other], axis=1), jnp.stack([other, kept], axis=1))
    arrived = [lax.dynamic_index_in_dim(both, turn, 0, keepdims=False)]
    for step in range(1, turns):
        target = lax.dynamic_index_in_dim(both, (turn - step) % turns, 0, keepdims=False)
        arrived.append(lax.ppermute(target, "group", [(i, (i - 2 * step) % groups) for i in range(groups)]))
    ring = jnp.stack(arrived + arrived[:-1], axis=0)
    ring = lax.dynamic_slice_in_dim(ring, (turns - turn) % turns, turns, 0)
    return ring.reshape(groups * row_order.size, col_order.size)


def body(residual_in, local_inverse, coarse_inverse, cluster_of, margin_peer, margin_row):
    rhs, comps, own = residual_in.shape
    over = margin_row.shape[0]
    subs = lax.axis_size("sub")
    groups = lax.axis_size("group")
    cl_dev = coarse_inverse.shape[0] // comps
    width = local_inverse.shape[1]
    m = make(rhs, comps, own, over, subs, groups, cl_dev)
    slots, lanes, block, main, tail = m["slots"], m["lanes"], m["block"], m["main"], m["tail"]
    each = main * ROWS
    inverse = local_inverse.reshape(comps, 2, own, width)
    row_of = lambda values: values.reshape(1, -1)

    def swap(send):
        return exchange(send.reshape(subs, ROWS, send.shape[1]), "sub").reshape(send.shape)

    whole = lambda shape: pl.BlockSpec(shape, lambda step: (0,) * len(shape))
    part_of = lambda which: pl.BlockSpec((comps // 3, 1, own, width), lambda step: (step, which, 0, 0))
    vmem = lambda shape, dtype: pltpu.VMEM(shape, dtype)

    with jax.named_scope("begin"):
        field, field16, fieldr, send, own8, own8t, own_tail, own_kind, take, take_t = kernel_call(
            m["begin"],
            [
                ((own, lanes), F32),
                ((own, lanes), BF16),
                ((rhs, lanes), BF16),
                ((slots, block), BF16),
                ((slots, own), BF16),
                ((own, slots), BF16),
                ((tail * own, slots), BF16),
                ((own, LANES), F32),
                ((over, slots), BF16),
                ((slots, over), BF16),
            ],
            residual_in,
            row_of(cluster_of),
            row_of(margin_peer),
            row_of(margin_row),
        )
    with jax.named_scope("regroup"):
        coarse_inverse, send = lax.optimization_barrier((coarse_inverse, send))
        matrix = regroup(coarse_inverse, groups, subs, cl_dev, comps)
    with jax.named_scope("answer"):
        got = swap(send)
        send, give, give_t, members = kernel_call(
            m["answer"],
            [((slots, lanes + block), BF16), ((slots, own), BF16), ((own, slots), BF16), ((ROWS, block), F32)],
            got,
            field16,
            row_of(cluster_of),
        )
    with jax.named_scope("own_half_first"):
        fieldr, send = lax.optimization_barrier((fieldr, send))
        part = kernel_call(
            m["half"],
            [((rhs, width), F32)],
            fieldr,
            inverse,
            grid=(3,),
            in_specs=[whole((rhs, lanes)), part_of(0)],
            out_specs=[whole((rhs, width))],
        )[0]
    got = swap(send)

    def coarse_parts(got, offset, rows, inner):
        return exchange(
            kernel_call(
                functools.partial(m["coarse"], offset, rows), [((groups, rows, LANES), BF16)], matrix, got, *inner
            )[0],
            "group",
        )

    def finish(full, got, part):
        sent = lanes + block if full else lanes
        return kernel_call(
            functools.partial(m["finish"], full),
            [((own, lanes), F32), ((slots, sent), BF16)],
            got,
            part,
            inverse,
            take,
            take_t,
            own8,
            grid=(3,),
            in_specs=[
                whole(got.shape),
                whole((rhs, width)),
                part_of(1),
                whole((over, slots)),
                whole((slots, over)),
                whole((slots, own)),
            ],
            out_specs=[whole((own, lanes)), whole((slots, sent))],
            scratch_shapes=[
                vmem((rhs, lanes), BF16),
                vmem((rhs, width), F32),
                vmem((own, lanes), BF16),
                vmem((over, lanes), BF16),
            ],
        )

    with jax.named_scope("coarse_first"):
        parts = coarse_parts(got, lanes, each, [])
    with jax.named_scope("solve_first"):
        res_own, sent = finish(True, got, part)
    with jax.named_scope("return_first"):
        send, sol = kernel_call(
            m["join_first"], [((slots, lanes + 2 * block), BF16), ((ROWS, block), F32)], sent, parts
        )
        got = swap(send)
    with jax.named_scope("combine"):
        first, send = kernel_call(
            m["combine"],
            [((own, lanes), F32), ((slots, lanes + block), BF16)],
            got, res_own, give, give_t, own8t, own_tail, own_kind, members, sol,
        )
    with jax.named_scope("own_half_second"):
        got = swap(send)
        first_out, inner, part = kernel_call(
            m["half_first"],
            [((rhs, comps, own), F32), ((2, LANES), F32), ((rhs, width), F32)],
            first,
            field,
            inverse,
            grid=(3,),
            in_specs=[whole((own, lanes)), whole((own, lanes)), part_of(0)],
            out_specs=[whole((rhs, comps, own)), whole((2, LANES)), whole((rhs, width))],
            scratch_shapes=[vmem((rhs, lanes), BF16)],
        )
    with jax.named_scope("coarse_second"):
        parts = coarse_parts(got, lanes, each + 16, [inner])
    with jax.named_scope("solve_second"):
        res_own, sent = finish(False, got, part)
    with jax.named_scope("return_second"):
        send = kernel_call(m["join_second"], [((slots, lanes + block), BF16)], sent, parts)[0]
        got = swap(send)
    with jax.named_scope("end"):
        second = kernel_call(
            m["end"], [((rhs, comps, own), F32)], got, res_own, first, give_t, own8t, own_tail, own_kind
        )[0]
    return first_out, second


def solution(mesh):
    placed = (
        P(None, None, ("group", "sub")),
        P(("group", "sub"), None, None),
        P(("group", "sub"), None),
        P(("group", "sub")),
        P(("group", "sub"), None),
        P(("group", "sub")),
    )
    return jax.shard_map(
        body,
        mesh=mesh,
        in_specs=placed,
        out_specs=(P(None, None, ("group", "sub")), P(None, None, ("group", "sub"))),
        check_vma=False,
    )
```

```python
import functools

import jax
import jax.numpy as jnp
import numpy as np
from jax import lax
from jax.experimental import pallas as pl
from jax.experimental.pallas import tpu as pltpu
from jax.sharding import PartitionSpec as P

EPSILON = 1e-06
F32 = jnp.float32
BF16 = jnp.bfloat16
LANES = 128
ROWS = 8
RING = 4


def dot(left, right):
    return jnp.dot(left, right, preferred_element_type=F32)


def exchange(values, axis):
    return lax.all_to_all(values, axis, split_axis=0, concat_axis=0, tiled=True)


def tile(values, index):
    return values[:, index * LANES : (index + 1) * LANES]


def iota(shape, axis):
    return lax.broadcasted_iota(jnp.int32, shape, axis)


def over_rows(values, subs):
    cube = values.reshape(subs, ROWS, LANES)
    return jnp.broadcast_to(jnp.sum(cube, axis=1, keepdims=True), cube.shape).reshape(subs * ROWS, LANES)


def one_row(values, row, subs):
    cube = values.reshape(subs, ROWS, LANES)
    return jnp.broadcast_to(cube[:, row : row + 1, :], cube.shape).reshape(subs * ROWS, LANES)


def repeat_rows(values, subs):
    return jnp.broadcast_to(values[None], (subs,) + values.shape).reshape(subs * ROWS, values.shape[1])


def kernel_call(body, outs, *args, flops=0, moved=0, limit=48, after=(), in_specs=None, **kw):
    count = len(after)
    specs = in_specs or [pl.BlockSpec(memory_space=pltpu.VMEM)] * len(args)
    return pl.pallas_call(
        lambda *refs: body(*refs[count:]),
        out_shape=[jax.ShapeDtypeStruct(shape, dtype) for shape, dtype in outs],
        in_specs=[pl.BlockSpec(memory_space=pl.ANY)] * count + list(specs),
        compiler_params=pltpu.CompilerParams(vmem_limit_bytes=limit * 1024 * 1024),
        cost_estimate=pl.CostEstimate(flops=flops, bytes_accessed=moved, transcendentals=0),
        **kw,
    )(*after, *args)


def make(rhs, comps, own, over, subs, groups, cl_dev):
    tail = ROWS - cl_dev
    main = comps - tail
    slots = subs * ROWS
    lanes = comps * LANES
    block = main * LANES
    share = -(-main // RING) * LANES
    aux = main - 1
    at_take, at_own, at_tail = 0, over, over + own
    at_kind = at_tail + tail * own
    at_rows = at_kind + own
    map_rows = at_rows + slots

    def pack(sums, extra, ref, offset):
        inner = iota((slots, LANES), 0) % ROWS
        for t in range(main):
            value = tile(sums, t)
            if t < cl_dev:
                for j in range(tail):
                    value = jnp.where(inner == cl_dev + j, one_row(tile(sums, main + j), t, subs), value)
            elif extra is not None:
                value = jnp.where(inner == cl_dev, extra, value)
            ref[:, offset + t * LANES : offset + (t + 1) * LANES] = value.astype(BF16)

    def prolong(tiles, own8t, own_tail, own_kind):
        head = dot(own8t, tiles)
        picked = dot(own_tail, tiles[:, : cl_dev * LANES])
        parts = [head]
        for j in range(tail):
            rows = picked[j * own : (j + 1) * own]
            value = jnp.zeros((own, LANES), F32)
            for t in range(cl_dev):
                value = jnp.where(own_kind == t, tile(rows, t), value)
            parts.append(value)
        return jnp.concatenate(parts, axis=1)

    def places(cl, peer):
        number = cl[...]
        holder = ((number.astype(F32) + 0.5) * (1.0 / cl_dev)).astype(jnp.int32)
        kind = number - holder * cl_dev
        rows = iota((slots, own), 0)
        hot = (rows == holder * ROWS + kind).astype(F32)
        peers = jnp.broadcast_to(peer[...].astype(F32), (over, over))
        same = (peers == peers.T) & (iota((over, over), 0) < iota((over, over), 1))
        rank = jnp.sum(same.astype(F32), axis=0, keepdims=True).astype(jnp.int32)
        dest = peer[...] * ROWS + rank
        hot_dest = (iota((slots, over), 0) == dest).astype(F32)
        return rows, holder, kind, hot, hot_dest

    def begin(res_hbm, cl_hbm, peer_hbm, row_hbm, send, token, res, cl, peer, row, field16, sems):
        token[...] = jnp.zeros((ROWS, LANES), F32)
        pairs = [(peer_hbm, peer), (row_hbm, row), (cl_hbm, cl), (res_hbm, res)]
        copies = [pltpu.make_async_copy(src, dst, sems.at[i]) for i, (src, dst) in enumerate(pairs)]
        for copy in copies:
            copy.start()
        for copy in copies[:3]:
            copy.wait()
        rows, holder, kind, hot, hot_dest = places(cl, peer)
        inner = rows % ROWS
        lane = iota((slots, LANES), 1)
        wanted = jnp.sum(hot_dest * (row[...] + 1).astype(F32), axis=1, keepdims=True)
        counts = jnp.sum(hot, axis=1, keepdims=True)
        extra = jnp.where(lane == inner, wanted, 0.0) + jnp.where(lane == inner + ROWS, counts, 0.0)
        copies[3].wait()
        for k in range(comps):
            field16[:, k * LANES : (k + 1) * LANES] = res[k].T.astype(BF16)
        pack(dot(hot.astype(BF16), field16[...]), over_rows(extra, subs), send, 0)

    def keep_maps(res, cl, peer, field16, maps):
        for k in range(comps):
            field16[:, k * LANES : (k + 1) * LANES] = res[k].T.astype(BF16)
        rows, holder, kind, hot, hot_dest = places(cl, peer)
        maps[at_take : at_take + over, :] = hot_dest.T.astype(BF16)
        cluster_maps(holder, kind, maps, at_own)
        maps[at_rows : at_rows + slots, :over] = hot_dest.astype(BF16)
        maps[at_rows : at_rows + slots, over : over + own] = hot.astype(BF16)

    def asking(got):
        lane = iota((slots, LANES), 1)
        inner = iota((slots, LANES), 0) % ROWS
        asked = one_row(tile(got, aux).astype(F32), cl_dev, subs)
        asked = jnp.sum(jnp.where(lane == inner, asked, 0.0), axis=1, keepdims=True) - 1.0
        hot = (iota((slots, own), 1).astype(F32) == asked).astype(F32)
        return lane, inner, hot

    def answer(got, field16, cl, send, token):
        token[...] = jnp.zeros((ROWS, LANES), F32)
        total = jnp.sum(got[...].astype(F32).reshape(subs, ROWS, block), axis=0)
        lane, inner, hot = asking(got)
        send[:, :lanes] = dot(hot.astype(BF16), field16[...]).astype(BF16)
        ids = jnp.sum(hot * cl[...].astype(F32), axis=1, keepdims=True)
        ids = over_rows(jnp.where(lane == inner, ids, 0.0), subs)
        for t in range(main):
            value = repeat_rows(tile(total, t), subs)
            if t >= cl_dev:
                value = jnp.where(inner == cl_dev, ids, value)
            send[:, lanes + t * LANES : lanes + (t + 1) * LANES] = value.astype(BF16)

    def keep_answer(got, gives, gives_late, members):
        lane, inner, hot = asking(got)
        gives_late[...] = hot.T.astype(BF16)
        gives[:own, :] = hot.T.astype(BF16)
        gives[own:, :own] = hot.astype(BF16)
        gives[own:, own:] = jnp.zeros((slots, slots - own), BF16)
        total = jnp.sum(tile(got, aux).astype(F32).reshape(subs, ROWS, LANES), axis=0)
        small = iota((ROWS, LANES), 0)
        small_lane = iota((ROWS, LANES), 1)
        numbers = [
            jnp.sum(jnp.where((small_lane == ROWS + c) & (small == cl_dev), total, 0.0), axis=(0, 1), keepdims=True)
            for c in range(cl_dev)
        ]
        base = jnp.zeros((ROWS, LANES), F32)
        for c in range(cl_dev):
            base = jnp.where(small == c, numbers[c], base)
        for t in range(main):
            count = jnp.where(small < cl_dev, base, numbers[t]) if t < cl_dev else base
            members[:, t * LANES : (t + 1) * LANES] = count

    def gather(place, *refs):
        pieces, outs = refs[:-2], refs[-2:]
        turns = len(pieces)
        sides = pieces[0].shape[0]
        for step, piece in enumerate(pieces):
            turn = place[0, 1] + step
            turn = jnp.where(turn >= turns, turn - turns, turn)
            for side in range(sides):
                core = place[0, 0] if side == 0 else 1 - place[0, 0]
                for out in outs:
                    out[sides * turn + core] = piece[side]

    def coarse(offset, rows, matrix, got, *refs):
        out = refs[-1]
        each = main * ROWS
        total = jnp.zeros((groups * each, LANES), F32)
        for t in range(main):
            columns = matrix[:, :, t * slots : (t + 1) * slots].reshape(groups * each, slots)
            total += dot(columns, got[:, offset + t * LANES : offset + (t + 1) * LANES])
        for g in range(groups):
            out[g, :each, :] = total[g * each : (g + 1) * each].astype(BF16)
        if rows > each:
            inner = refs[0][...]
            high = inner.astype(BF16).astype(F32)
            last = jnp.concatenate([high, inner - high, jnp.zeros((rows - each - 4, LANES), F32)], axis=0)
            for g in range(groups):
                out[g, each:, :] = last.astype(BF16)

    def group_total(got):
        total = jnp.sum(got[...].astype(F32), axis=0)
        return total, [total[t * ROWS : (t + 1) * ROWS] for t in range(main)]

    def loads(inverse, which, buffer, sems):
        copies = [pltpu.make_async_copy(inverse.at[k, which], buffer.at[k], sems.at[k]) for k in range(comps)]
        for copy in copies:
            copy.start()
        return copies

    def product(copies, turned, buffer, part, out):
        third = comps // 3
        for step in range(3):
            for copy in copies[step * third : (step + 1) * third]:
                copy.wait()
            rows = buffer[step * third : (step + 1) * third].reshape(third * own, out.shape[1])
            value = dot(turned[:, step * third * LANES : (step + 1) * third * LANES], rows)
            if step:
                out[...] += value
            elif part is None:
                out[...] = value
            else:
                out[...] = part[...] + value

    def half(res, inverse, out, token, turned, buffer, sems):
        token[...] = jnp.zeros((ROWS, LANES), F32)
        copies = loads(inverse, 0, buffer, sems)
        for k in range(comps):
            turned[:, k * LANES : (k + 1) * LANES] = res[k].astype(BF16)
        product(copies, turned, buffer, None, out)

    def half_first(place, spread, maps, over_maps, res, inverse, *refs):
        pieces, refs = refs[:RING], refs[RING:]
        first_out, inner, out, over_add, turned, buffer, sems, tiles = refs
        copies = loads(inverse, 0, buffer, sems)
        for step, piece in enumerate(pieces):
            member = place[0, 2] + step
            member = jnp.where(member >= RING, member - RING, member)

            @pl.when(member * share < block)
            def _(piece=piece, member=member):
                tiles[:, pl.ds(pl.multiple_of(member * share, LANES), share)] = piece[...]

        everything = tiles[...]
        values = spread[...] + prolong_maps(everything, maps, at_own)
        over_add[...] = prolong_maps(everything, over_maps, 0)
        rf = jnp.zeros((rhs, own), F32)
        ff = jnp.zeros((rhs, own), F32)
        for k in range(comps):
            flipped = tile(values, k).T
            first_out[k] = flipped
            turned[:, k * LANES : (k + 1) * LANES] = flipped.astype(BF16)
            rf += res[k] * flipped
            ff += flipped * flipped
        inner[0:1, :] = jnp.sum(rf.T, axis=0, keepdims=True)
        inner[1:2, :] = jnp.sum(ff.T, axis=0, keepdims=True)
        product(copies, turned, buffer, None, out)

    def solve(got, part, maps, inverse, *refs):
        extra, (out, turned, buffer, sems) = refs[:-4], refs[-4:]
        copies = loads(inverse, 1, buffer, sems)
        arrived = dot(maps[at_take : at_take + over, :], got[:, :lanes])
        for each_extra in extra:
            arrived += each_extra[...]
        for k in range(comps):
            turned[:, k * LANES : (k + 1) * LANES] = tile(arrived, k).T.astype(BF16)
        product(copies, turned, buffer, part, out)

    def finish_first(got, total, parts, maps, send, res_own, over_maps, sol, token, own16, over16):
        token[...] = jnp.zeros((ROWS, LANES), F32)
        cams = own + over
        for k in range(comps):
            flipped = total[:, k * cams : (k + 1) * cams].T
            res_own[:, k * LANES : (k + 1) * LANES] = flipped[:own]
            flipped = flipped.astype(BF16)
            own16[:, k * LANES : (k + 1) * LANES] = flipped[:own]
            over16[:, k * LANES : (k + 1) * LANES] = flipped[own:]
        rows = maps[at_rows : at_rows + slots, :]
        take_t, own8 = rows[:, :over], rows[:, over : over + own]
        send[:, :lanes] = dot(take_t, over16[...]).astype(BF16)
        holder, kind = margin_places(got, take_t)
        cluster_maps(holder, kind, over_maps, 0)
        over8 = (iota((slots, over), 0) == holder * ROWS + kind).astype(F32).astype(BF16)
        pack(dot(own8, own16[...]) + dot(over8, over16[...]), None, send, lanes)
        _, tiles = group_total(parts)
        each_share = share // LANES
        for t in range(main):
            sol[:, t * LANES : (t + 1) * LANES] = tiles[t]
        member = iota((slots, LANES), 0) // ROWS % RING
        for j in range(each_share):
            value = jnp.zeros((slots, LANES), F32)
            for q in range(RING):
                if q * each_share + j < main:
                    value = jnp.where(member == q, repeat_rows(tiles[q * each_share + j], subs), value)
            at = lanes + block + j * LANES
            send[:, at : at + LANES] = value.astype(BF16)

    def margin_places(got, take_t):
        lane = iota((slots, LANES), 1)
        inner = iota((slots, LANES), 0) % ROWS
        ids = one_row(got[:, lanes + aux * LANES : lanes + (aux + 1) * LANES].astype(F32), cl_dev, subs)
        ids = jnp.sum(jnp.where(lane == inner, ids, 0.0), axis=1, keepdims=True)
        number = jnp.sum(take_t.astype(F32) * ids, axis=0, keepdims=True)
        holder = ((number + 0.5) * (1.0 / cl_dev)).astype(jnp.int32)
        return holder, number.astype(jnp.int32) - holder * cl_dev

    def cluster_maps(holder, kind, maps, base):
        rows = iota((slots, own), 0)
        hot = (rows == holder * ROWS + kind).astype(F32)
        maps[base : base + own, :] = hot.T.astype(BF16)
        for j in range(tail):
            hot_j = (rows == holder * ROWS + (cl_dev + j)).astype(F32)
            maps[base + (1 + j) * own : base + (2 + j) * own, :] = hot_j.T.astype(BF16)
        at = base + (1 + tail) * own
        maps[at : at + own, :] = jnp.broadcast_to(kind.astype(F32), (slots, own)).T.astype(BF16)

    def finish_second(total, parts, maps, send, res_own, over16):
        cams = own + over
        for k in range(comps):
            flipped = total[:, k * cams : (k + 1) * cams].T
            res_own[:, k * LANES : (k + 1) * LANES] = flipped[:own]
            over16[:, k * LANES : (k + 1) * LANES] = flipped[own:].astype(BF16)
        send[:, :lanes] = dot(maps[at_rows : at_rows + slots, :over], over16[...]).astype(BF16)
        summed, tiles = group_total(parts)
        each = main * ROWS
        inner = summed[each : each + 2] + summed[each + 2 : each + 4]
        small = iota((ROWS, LANES), 0)
        for t in range(main):
            value = tiles[t]
            if t == aux:
                value = jnp.where(small == cl_dev, inner[0:1], value)
                value = jnp.where(small == cl_dev + 1, inner[1:2], value)
            send[:, lanes + t * LANES : lanes + (t + 1) * LANES] = repeat_rows(value, subs).astype(BF16)

    def prolong_maps(tiles, maps, base):
        kind = maps[base + (1 + tail) * own : base + (2 + tail) * own, :LANES].astype(F32)
        return prolong(tiles, maps[base : base + own, :], maps[base + own : base + (1 + tail) * own, :], kind)

    def combine(got, res_own, gives, members, sol, send, third, spread, token):
        token[...] = jnp.zeros((ROWS, LANES), F32)
        values = res_own[...] + dot(gives[:own, :], got[:, :lanes])
        spread[...] = values
        send[:, :lanes] = dot(gives[own:, :own], values.astype(BF16)).astype(BF16)
        total = jnp.sum(got[:, lanes : lanes + block].astype(F32).reshape(subs, ROWS, block), axis=0)
        for t in range(main):
            columns = slice(t * LANES, (t + 1) * LANES)
            value = tile(total, t) + members[:, columns] * sol[:, columns]
            send[:, lanes + t * LANES : lanes + (t + 1) * LANES] = repeat_rows(value, subs).astype(BF16)
        third[...] = got[:, lanes + block :]

    def end(got, res_own, first, gives, maps, out):
        applied = res_own[...] + dot(gives[...], got[:, :lanes])
        applied += prolong_maps(got[:, lanes:], maps, at_own)
        sums = got[:, lanes + aux * LANES :].astype(F32).reshape(subs, ROWS, LANES)
        sums = jnp.sum(sums, axis=0)
        scale = sums[cl_dev : cl_dev + 1] / (sums[cl_dev + 1 : cl_dev + 2] + EPSILON)
        for k in range(comps):
            out[k] = first[k] - (scale * tile(applied, k)).T

    return dict(locals())


def block_order(cl_dev, comps, count):
    tail = ROWS - cl_dev
    main = comps - tail
    order = np.full((main, count, ROWS), -1, np.int32)
    for t in range(main):
        for i in range(ROWS):
            if i < cl_dev:
                order[t, :, i] = np.arange(count) * cl_dev * comps + i * comps + t
            elif t < cl_dev:
                order[t, :, i] = np.arange(count) * cl_dev * comps + t * comps + main + i - cl_dev
    return order.reshape(-1)


def regroup(coarse_inverse, groups, subs, cl_dev, comps):
    cl_rows = cl_dev * comps
    grp_rows = cl_rows * subs
    row_order = block_order(cl_dev, comps, 1)
    col_order = block_order(cl_dev, comps, subs)
    pick_rows = jnp.asarray(row_order[:, None] == np.arange(cl_rows)[None, :]).astype(BF16)
    pick_cols = (jnp.asarray(col_order)[None, :] == jnp.arange(grp_rows, dtype=jnp.int32)[:, None]).astype(BF16)
    values = coarse_inverse.reshape(cl_rows, groups, grp_rows)
    values = lax.dot_general(pick_rows, values, (((1,), (0,)), ((), ())), preferred_element_type=F32).astype(BF16)
    values = values.transpose(1, 0, 2).reshape(groups * row_order.size, grp_rows)
    return dot(values, pick_cols).astype(BF16).reshape(groups, row_order.size, col_order.size)


def place_of():
    index = lax.axis_index("group")
    return index % 2, index // 2


def pass_round(values, after):
    groups = values.shape[0]
    if groups == 1:
        return [values]
    turns = groups // 2
    core, turn = place_of()
    pairs = values.reshape((turns, 2) + values.shape[1:])
    kept = lax.dynamic_index_in_dim(pairs, core, 1, keepdims=False)
    given = lax.dynamic_index_in_dim(pairs, 1 - core, 1, keepdims=False)
    given, after = lax.optimization_barrier((given, after))
    other = lax.ppermute(given, "group", [(i, i ^ 1) for i in range(groups)])
    pieces = []
    for step in range(turns):
        target = (turn - step) % turns
        piece = jnp.stack([lax.dynamic_index_in_dim(part, target, 0, keepdims=False) for part in (kept, other)])
        if step:
            piece = lax.ppermute(piece, "group", [(i, (i - 2 * step) % groups) for i in range(groups)])
        pieces.append(piece)
    return pieces


def body(residual_in, local_inverse, coarse_inverse, cluster_of, margin_peer, margin_row):
    rhs, comps, own = residual_in.shape
    over = margin_row.shape[0]
    subs = lax.axis_size("sub")
    groups = lax.axis_size("group")
    cl_dev = coarse_inverse.shape[0] // comps
    width = local_inverse.shape[1]
    m = make(rhs, comps, own, over, subs, groups, cl_dev)
    slots, lanes, block, main, tail = m["slots"], m["lanes"], m["block"], m["main"], m["tail"]
    share = m["share"]
    each = main * ROWS
    inverse = local_inverse.reshape(comps, 2, own, width)
    residual = residual_in.transpose(1, 0, 2)
    cluster, peer, row = [values.reshape(1, -1) for values in (cluster_of, margin_peer, margin_row)]
    hbm = pl.BlockSpec(memory_space=pltpu.HBM)
    here = pl.BlockSpec(memory_space=pltpu.VMEM)
    vmem = pltpu.VMEM
    half_cost = dict(flops=rhs * width * width, moved=width * width)
    mark = ((ROWS, LANES), F32)
    half_scratch = [
        vmem((rhs, lanes), BF16),
        vmem((comps, own, width), BF16),
        pltpu.SemaphoreType.DMA((comps,)),
    ]

    def swap(send):
        return exchange(send.reshape(subs, ROWS, send.shape[1]), "sub").reshape(send.shape)

    def coarse_parts(matrix, got, rows, inner, after=()):
        parts = kernel_call(
            functools.partial(m["coarse"], lanes, rows),
            [((groups, rows, LANES), BF16)],
            matrix,
            got,
            *inner,
            after=after,
        )[0]
        return exchange(parts, "group")

    def solve(got, part, *extra):
        return kernel_call(
            m["solve"],
            [((rhs, width), F32)],
            got,
            part,
            maps,
            inverse,
            *extra,
            in_specs=[here, here, here, hbm] + [here] * len(extra),
            scratch_shapes=half_scratch,
            limit=48,
            **half_cost,
        )[0]

    with jax.named_scope("begin"):
        send, token = kernel_call(
            m["begin"],
            [((slots, block), BF16), mark],
            residual,
            cluster,
            peer,
            row,
            in_specs=[hbm] * 4,
            limit=60,
            scratch_shapes=[
                vmem((comps, rhs, own), F32),
                vmem((1, own), jnp.int32),
                vmem((1, over), jnp.int32),
                vmem((1, over), jnp.int32),
                vmem((own, lanes), BF16),
                pltpu.SemaphoreType.DMA((4,)),
            ],
        )
    with jax.named_scope("maps"):
        field16, maps = kernel_call(
            m["keep_maps"],
            [((own, lanes), BF16), ((m["map_rows"], slots), BF16)],
            residual,
            cluster,
            peer,
            after=[token],
        )
    with jax.named_scope("regroup"):
        matrix = regroup(coarse_inverse, groups, subs, cl_dev, comps)
        member = lax.axis_index("sub") % RING
        place = jnp.stack((place_of() if groups > 1 else (0, 0)) + (member,)).astype(jnp.int32).reshape(1, 3)
    with jax.named_scope("answer"):
        got = swap(send)
        send, token = kernel_call(
            m["answer"], [((slots, lanes + block), BF16), mark], got, field16, cluster
        )
        gives, gives_late, members = kernel_call(
            m["keep_answer"],
            [((own + slots, slots), BF16), ((own, slots), BF16), ((ROWS, block), F32)],
            got,
            after=[token],
        )
    with jax.named_scope("own_half_first"):
        part, half_token = kernel_call(
            m["half"],
            [((rhs, width), F32), mark],
            residual,
            inverse,
            after=[token],
            in_specs=[here, hbm],
            scratch_shapes=half_scratch,
            **half_cost,
        )
    with jax.named_scope("regroup"):
        pieces = pass_round(matrix, token)
        matrix, matrix_late = kernel_call(
            m["gather"],
            [(matrix.shape, BF16)] * 2,
            place,
            *pieces,
            after=[half_token],
            in_specs=[pl.BlockSpec(memory_space=pltpu.SMEM)] + [here] * len(pieces),
        )
    got = swap(send)

    with jax.named_scope("coarse_first"):
        parts = coarse_parts(matrix, got, each, [], [half_token, members])
    with jax.named_scope("solve_first"):
        total = solve(got, part)
    with jax.named_scope("return_first"):
        send, res_own, over_maps, sol, token = kernel_call(
            m["finish_first"],
            [
                ((slots, lanes + block + share), BF16),
                ((own, lanes), F32),
                (((2 + tail) * own, slots), BF16),
                ((ROWS, block), F32),
                mark,
            ],
            got,
            total,
            parts,
            maps,
            scratch_shapes=[vmem((own, lanes), BF16), vmem((over, lanes), BF16)],
        )
        got = swap(send)
    with jax.named_scope("combine"):
        send, third, spread, token = kernel_call(
            m["combine"],
            [((slots, lanes + block), BF16), ((slots, share), BF16), ((own, lanes), F32), mark],
            got,
            res_own,
            gives,
            members,
            sol,
        )
    with jax.named_scope("own_half_second"):
        pieces_x = [third]
        for step in range(1, RING):
            turn = [(i, i // RING * RING + (i - step) % RING) for i in range(subs)]
            pieces_x.append(lax.ppermute(third, "sub", turn))
        first, inner, part, over_add = kernel_call(
            m["half_first"],
            [((comps, rhs, own), F32), ((2, LANES), F32), ((rhs, width), F32), ((over, lanes), F32)],
            place,
            spread,
            maps,
            over_maps,
            residual,
            inverse,
            *pieces_x,
            after=[token],
            in_specs=[pl.BlockSpec(memory_space=pltpu.SMEM)] + [here] * 4 + [hbm] + [here] * RING,
            scratch_shapes=half_scratch + [vmem((slots, block), BF16)],
            limit=48,
            **half_cost,
        )
    got = swap(send)
    with jax.named_scope("coarse_second"):
        parts = coarse_parts(matrix_late, got, each + 16, [inner])
    with jax.named_scope("solve_second"):
        total = solve(got, part, over_add)
    with jax.named_scope("return_second"):
        send, res_own = kernel_call(
            m["finish_second"],
            [((slots, lanes + block), BF16), ((own, lanes), F32)],
            total,
            parts,
            maps,
            scratch_shapes=[vmem((over, lanes), BF16)],
        )
        got = swap(send)
    with jax.named_scope("end"):
        second = kernel_call(m["end"], [((comps, rhs, own), F32)], got, res_own, first, gives_late, maps)[0]
    return first.transpose(1, 0, 2), second.transpose(1, 0, 2)


def solution(mesh):
    placed = (
        P(None, None, ("group", "sub")),
        P(("group", "sub"), None, None),
        P(("group", "sub"), None),
        P(("group", "sub")),
        P(("group", "sub"), None),
        P(("group", "sub")),
    )
    return jax.shard_map(
        body,
        mesh=mesh,
        in_specs=placed,
        out_specs=(P(None, None, ("group", "sub")), P(None, None, ("group", "sub"))),
        check_vma=False,
    )
```

```python
import functools

import jax
import jax.numpy as jnp
from jax import lax
from jax.experimental import pallas as pl
from jax.experimental.pallas import tpu as pltpu
from jax.sharding import PartitionSpec as P

EPSILON = 1e-06
F32 = jnp.float32
BF16 = jnp.bfloat16
LANES = 128
ROWS = 8
RING = 4


def dot(left, right):
    return jnp.dot(left, right, preferred_element_type=F32)


def exchange(values, axis):
    return lax.all_to_all(values, axis, split_axis=0, concat_axis=0, tiled=True)


def tile(values, index):
    return values[:, index * LANES : (index + 1) * LANES]


def iota(shape, axis):
    return lax.broadcasted_iota(jnp.int32, shape, axis)


def over_rows(values, subs):
    cube = values.reshape(subs, ROWS, LANES)
    return jnp.broadcast_to(jnp.sum(cube, axis=1, keepdims=True), cube.shape).reshape(subs * ROWS, LANES)


def one_row(values, row, subs):
    cube = values.reshape(subs, ROWS, LANES)
    return jnp.broadcast_to(cube[:, row : row + 1, :], cube.shape).reshape(subs * ROWS, LANES)


def repeat_rows(values, subs):
    return jnp.broadcast_to(values[None], (subs,) + values.shape).reshape(subs * ROWS, values.shape[1])


def kernel_call(body, outs, *args, flops=0, moved=0, limit=48, after=(), in_specs=None, **kw):
    count = len(after)
    specs = in_specs or [pl.BlockSpec(memory_space=pltpu.VMEM)] * len(args)
    return pl.pallas_call(
        lambda *refs: body(*refs[count:]),
        out_shape=[jax.ShapeDtypeStruct(shape, dtype) for shape, dtype in outs],
        in_specs=[pl.BlockSpec(memory_space=pl.ANY)] * count + list(specs),
        compiler_params=pltpu.CompilerParams(vmem_limit_bytes=limit * 1024 * 1024),
        cost_estimate=pl.CostEstimate(flops=flops, bytes_accessed=moved, transcendentals=0),
        **kw,
    )(*after, *args)


def make(rhs, comps, own, over, subs, groups, cl_dev):
    tail = ROWS - cl_dev
    main = comps - tail
    slots = subs * ROWS
    lanes = comps * LANES
    block = main * LANES
    share = -(-main // RING) * LANES
    aux = main - 1
    at_take, at_own, at_tail = 0, over, over + own
    at_kind = at_tail + tail * own
    at_rows = at_kind + own
    map_rows = at_rows + slots

    def pack(sums, extra, ref, offset):
        inner = iota((slots, LANES), 0) % ROWS
        for t in range(main):
            value = tile(sums, t)
            if t < cl_dev:
                for j in range(tail):
                    value = jnp.where(inner == cl_dev + j, one_row(tile(sums, main + j), t, subs), value)
            elif extra is not None:
                value = jnp.where(inner == cl_dev, extra, value)
            ref[:, offset + t * LANES : offset + (t + 1) * LANES] = value.astype(BF16)

    def prolong(tiles, own8t, own_tail, own_kind):
        head = dot(own8t, tiles)
        picked = dot(own_tail, tiles[:, : cl_dev * LANES])
        parts = [head]
        for j in range(tail):
            rows = picked[j * own : (j + 1) * own]
            value = jnp.zeros((own, LANES), F32)
            for t in range(cl_dev):
                value = jnp.where(own_kind == t, tile(rows, t), value)
            parts.append(value)
        return jnp.concatenate(parts, axis=1)

    def places(cl, peer):
        number = cl[...]
        holder = ((number.astype(F32) + 0.5) * (1.0 / cl_dev)).astype(jnp.int32)
        kind = number - holder * cl_dev
        rows = iota((slots, own), 0)
        hot = (rows == holder * ROWS + kind).astype(F32)
        peers = jnp.broadcast_to(peer[...].astype(F32), (over, over))
        same = (peers == peers.T) & (iota((over, over), 0) < iota((over, over), 1))
        rank = jnp.sum(same.astype(F32), axis=0, keepdims=True).astype(jnp.int32)
        dest = peer[...] * ROWS + rank
        hot_dest = (iota((slots, over), 0) == dest).astype(F32)
        return rows, holder, kind, hot, hot_dest

    def begin(res_hbm, cl_hbm, peer_hbm, row_hbm, send, token, res, cl, peer, row, field16, sems):
        token[...] = jnp.zeros((ROWS, LANES), F32)
        pairs = [(peer_hbm, peer), (row_hbm, row), (cl_hbm, cl), (res_hbm, res)]
        copies = [pltpu.make_async_copy(src, dst, sems.at[i]) for i, (src, dst) in enumerate(pairs)]
        for copy in copies:
            copy.start()
        for copy in copies[:3]:
            copy.wait()
        rows, holder, kind, hot, hot_dest = places(cl, peer)
        inner = rows % ROWS
        lane = iota((slots, LANES), 1)
        wanted = jnp.sum(hot_dest * (row[...] + 1).astype(F32), axis=1, keepdims=True)
        counts = jnp.sum(hot, axis=1, keepdims=True)
        extra = jnp.where(lane == inner, wanted, 0.0) + jnp.where(lane == inner + ROWS, counts, 0.0)
        copies[3].wait()
        for k in range(comps):
            field16[:, k * LANES : (k + 1) * LANES] = res[k].T.astype(BF16)
        pack(dot(hot.astype(BF16), field16[...]), over_rows(extra, subs), send, 0)

    def keep_maps(res, cl, peer, field16, maps):
        for k in range(comps):
            field16[:, k * LANES : (k + 1) * LANES] = res[k].T.astype(BF16)
        rows, holder, kind, hot, hot_dest = places(cl, peer)
        maps[at_take : at_take + over, :] = hot_dest.T.astype(BF16)
        cluster_maps(holder, kind, maps, at_own)
        maps[at_rows : at_rows + slots, :over] = hot_dest.astype(BF16)
        maps[at_rows : at_rows + slots, over : over + own] = hot.astype(BF16)

    def asking(got):
        lane = iota((slots, LANES), 1)
        inner = iota((slots, LANES), 0) % ROWS
        asked = one_row(tile(got, aux).astype(F32), cl_dev, subs)
        asked = jnp.sum(jnp.where(lane == inner, asked, 0.0), axis=1, keepdims=True) - 1.0
        hot = (iota((slots, own), 1).astype(F32) == asked).astype(F32)
        return lane, inner, hot

    def answer(got, field16, cl, send, token):
        token[...] = jnp.zeros((ROWS, LANES), F32)
        total = jnp.sum(got[...].astype(F32).reshape(subs, ROWS, block), axis=0)
        lane, inner, hot = asking(got)
        send[:, :lanes] = dot(hot.astype(BF16), field16[...]).astype(BF16)
        ids = jnp.sum(hot * cl[...].astype(F32), axis=1, keepdims=True)
        ids = over_rows(jnp.where(lane == inner, ids, 0.0), subs)
        for t in range(main):
            value = repeat_rows(tile(total, t), subs)
            if t >= cl_dev:
                value = jnp.where(inner == cl_dev, ids, value)
            send[:, lanes + t * LANES : lanes + (t + 1) * LANES] = value.astype(BF16)

    def keep_answer(got, gives, gives_late, members):
        lane, inner, hot = asking(got)
        gives_late[...] = hot.T.astype(BF16)
        gives[:own, :] = hot.T.astype(BF16)
        gives[own:, :own] = hot.astype(BF16)
        gives[own:, own:] = jnp.zeros((slots, slots - own), BF16)
        total = jnp.sum(tile(got, aux).astype(F32).reshape(subs, ROWS, LANES), axis=0)
        small = iota((ROWS, LANES), 0)
        small_lane = iota((ROWS, LANES), 1)
        numbers = [
            jnp.sum(jnp.where((small_lane == ROWS + c) & (small == cl_dev), total, 0.0), axis=(0, 1), keepdims=True)
            for c in range(cl_dev)
        ]
        base = jnp.zeros((ROWS, LANES), F32)
        for c in range(cl_dev):
            base = jnp.where(small == c, numbers[c], base)
        for t in range(main):
            count = jnp.where(small < cl_dev, base, numbers[t]) if t < cl_dev else base
            members[:, t * LANES : (t + 1) * LANES] = count

    def prepare(place, rows, kept, given, lined):
        cl_rows = cl_dev * comps
        grp_rows = cl_rows * subs
        each = main * ROWS
        window = main * slots
        turns = groups // 2
        at = iota((each, cl_rows), 0)
        t, i = at // ROWS, at % ROWS
        source = jnp.where(i < cl_dev, i * comps + t, t * comps + main + i - cl_dev)
        source = jnp.where((i < cl_dev) | (t < cl_dev), source, -1)
        pick = (source == iota((each, cl_rows), 1)).astype(F32).astype(BF16)
        for g in range(groups):
            start = g * grp_rows // LANES * LANES
            values = dot(pick, rows[:, start : start + window])
            shift = g * grp_rows - start
            if shift:
                values = pltpu.roll(values, window - shift, 1)
            lined[g] = values.astype(BF16)
        turned = []
        for side in range(2):
            parts = []
            for step in range(turns):
                turn = place[0, 1] - step
                turn = jnp.where(turn < 0, turn + turns, turn)
                core = place[0, 0] if side == 0 else 1 - place[0, 0]
                parts.append(lined[2 * turn + core])
            turned.append(jnp.concatenate(parts, axis=0))
        lane = iota((window, slots), 1)
        row = iota((window, slots), 0)
        holder, i = lane // ROWS, lane % ROWS
        for t in range(main):
            if t < cl_dev:
                source = holder * cl_rows + jnp.where(i < cl_dev, i * comps + t, t * comps + main + i - cl_dev)
            else:
                source = jnp.where(i < cl_dev, holder * cl_rows + i * comps + t, -1)
            moved = (source == row).astype(F32).astype(BF16)
            for values, out in zip(turned, (kept, given)):
                value = dot(values, moved).astype(BF16)
                for step in range(turns):
                    out[step, :, t * slots : (t + 1) * slots] = value[step * each : (step + 1) * each]

    def gather(place, own_piece, other_piece, *refs):
        pieces, outs = refs[:-2], refs[-2:]
        turns = len(pieces) + 1
        for step in range(turns):
            turn = place[0, 1] + step
            turn = jnp.where(turn >= turns, turn - turns, turn)
            for side in range(2):
                core = place[0, 0] if side == 0 else 1 - place[0, 0]
                value = pieces[step - 1][side] if step else (own_piece, other_piece)[side][...]
                for out in outs:
                    out[2 * turn + core] = value

    def coarse(offset, rows, matrix, got, *refs):
        out = refs[-1]
        each = main * ROWS
        total = jnp.zeros((groups * each, LANES), F32)
        for t in range(main):
            columns = matrix[:, :, t * slots : (t + 1) * slots].reshape(groups * each, slots)
            total += dot(columns, got[:, offset + t * LANES : offset + (t + 1) * LANES])
        for g in range(groups):
            out[g, :each, :] = total[g * each : (g + 1) * each].astype(BF16)
        if rows > each:
            inner = refs[0][...]
            high = inner.astype(BF16).astype(F32)
            last = jnp.concatenate([high, inner - high, jnp.zeros((rows - each - 4, LANES), F32)], axis=0)
            for g in range(groups):
                out[g, each:, :] = last.astype(BF16)

    def group_total(got):
        total = jnp.sum(got[...].astype(F32), axis=0)
        return total, [total[t * ROWS : (t + 1) * ROWS] for t in range(main)]

    def loads(inverse, which, buffer, sems):
        copies = [pltpu.make_async_copy(inverse.at[k, which], buffer.at[k], sems.at[k]) for k in range(comps)]
        for copy in copies:
            copy.start()
        return copies

    def product(copies, turned, buffer, part, out):
        third = comps // 3
        for step in range(3):
            for copy in copies[step * third : (step + 1) * third]:
                copy.wait()
            rows = buffer[step * third : (step + 1) * third].reshape(third * own, out.shape[1])
            value = dot(turned[:, step * third * LANES : (step + 1) * third * LANES], rows)
            if step:
                out[...] += value
            elif part is None:
                out[...] = value
            else:
                out[...] = part[...] + value

    def half(res, inverse, out, token, turned, buffer, sems):
        token[...] = jnp.zeros((ROWS, LANES), F32)
        copies = loads(inverse, 0, buffer, sems)
        for k in range(comps):
            turned[:, k * LANES : (k + 1) * LANES] = res[k].astype(BF16)
        product(copies, turned, buffer, None, out)

    def half_first(place, spread, maps, over_maps, res, inverse, *refs):
        pieces, refs = refs[:RING], refs[RING:]
        first_out, inner, out, over_add, turned, buffer, sems, tiles = refs
        copies = loads(inverse, 0, buffer, sems)
        for step, piece in enumerate(pieces):
            member = place[0, 2] + step
            member = jnp.where(member >= RING, member - RING, member)

            @pl.when(member * share < block)
            def _(piece=piece, member=member):
                tiles[:, pl.ds(pl.multiple_of(member * share, LANES), share)] = piece[...]

        everything = tiles[...]
        values = spread[...] + prolong_maps(everything, maps, at_own)
        over_add[...] = prolong_maps(everything, over_maps, 0)
        rf = jnp.zeros((rhs, own), F32)
        ff = jnp.zeros((rhs, own), F32)
        for k in range(comps):
            flipped = tile(values, k).T
            first_out[k] = flipped
            turned[:, k * LANES : (k + 1) * LANES] = flipped.astype(BF16)
            rf += res[k] * flipped
            ff += flipped * flipped
        inner[0:1, :] = jnp.sum(rf.T, axis=0, keepdims=True)
        inner[1:2, :] = jnp.sum(ff.T, axis=0, keepdims=True)
        product(copies, turned, buffer, None, out)

    def solve(got, part, maps, inverse, *refs):
        extra, (out, turned, buffer, sems) = refs[:-4], refs[-4:]
        copies = loads(inverse, 1, buffer, sems)
        arrived = dot(maps[at_take : at_take + over, :], got[:, :lanes])
        for each_extra in extra:
            arrived += each_extra[...]
        for k in range(comps):
            turned[:, k * LANES : (k + 1) * LANES] = tile(arrived, k).T.astype(BF16)
        product(copies, turned, buffer, part, out)

    def finish_first(got, total, parts, maps, send, res_own, over_maps, sol, token, own16, over16):
        token[...] = jnp.zeros((ROWS, LANES), F32)
        cams = own + over
        for k in range(comps):
            flipped = total[:, k * cams : (k + 1) * cams].T
            res_own[:, k * LANES : (k + 1) * LANES] = flipped[:own]
            flipped = flipped.astype(BF16)
            own16[:, k * LANES : (k + 1) * LANES] = flipped[:own]
            over16[:, k * LANES : (k + 1) * LANES] = flipped[own:]
        rows = maps[at_rows : at_rows + slots, :]
        take_t, own8 = rows[:, :over], rows[:, over : over + own]
        send[:, :lanes] = dot(take_t, over16[...]).astype(BF16)
        holder, kind = margin_places(got, take_t)
        cluster_maps(holder, kind, over_maps, 0)
        over8 = (iota((slots, over), 0) == holder * ROWS + kind).astype(F32).astype(BF16)
        pack(dot(own8, own16[...]) + dot(over8, over16[...]), None, send, lanes)
        _, tiles = group_total(parts)
        each_share = share // LANES
        for t in range(main):
            sol[:, t * LANES : (t + 1) * LANES] = tiles[t]
        member = iota((slots, LANES), 0) // ROWS % RING
        for j in range(each_share):
            value = jnp.zeros((slots, LANES), F32)
            for q in range(RING):
                if q * each_share + j < main:
                    value = jnp.where(member == q, repeat_rows(tiles[q * each_share + j], subs), value)
            at = lanes + block + j * LANES
            send[:, at : at + LANES] = value.astype(BF16)

    def margin_places(got, take_t):
        lane = iota((slots, LANES), 1)
        inner = iota((slots, LANES), 0) % ROWS
        ids = one_row(got[:, lanes + aux * LANES : lanes + (aux + 1) * LANES].astype(F32), cl_dev, subs)
        ids = jnp.sum(jnp.where(lane == inner, ids, 0.0), axis=1, keepdims=True)
        number = jnp.sum(take_t.astype(F32) * ids, axis=0, keepdims=True)
        holder = ((number + 0.5) * (1.0 / cl_dev)).astype(jnp.int32)
        return holder, number.astype(jnp.int32) - holder * cl_dev

    def cluster_maps(holder, kind, maps, base):
        rows = iota((slots, own), 0)
        hot = (rows == holder * ROWS + kind).astype(F32)
        maps[base : base + own, :] = hot.T.astype(BF16)
        for j in range(tail):
            hot_j = (rows == holder * ROWS + (cl_dev + j)).astype(F32)
            maps[base + (1 + j) * own : base + (2 + j) * own, :] = hot_j.T.astype(BF16)
        at = base + (1 + tail) * own
        maps[at : at + own, :] = jnp.broadcast_to(kind.astype(F32), (slots, own)).T.astype(BF16)

    def finish_second(total, parts, maps, send, res_own, over16):
        cams = own + over
        for k in range(comps):
            flipped = total[:, k * cams : (k + 1) * cams].T
            res_own[:, k * LANES : (k + 1) * LANES] = flipped[:own]
            over16[:, k * LANES : (k + 1) * LANES] = flipped[own:].astype(BF16)
        send[:, :lanes] = dot(maps[at_rows : at_rows + slots, :over], over16[...]).astype(BF16)
        summed, tiles = group_total(parts)
        each = main * ROWS
        inner = summed[each : each + 2] + summed[each + 2 : each + 4]
        small = iota((ROWS, LANES), 0)
        for t in range(main):
            value = tiles[t]
            if t == aux:
                value = jnp.where(small == cl_dev, inner[0:1], value)
                value = jnp.where(small == cl_dev + 1, inner[1:2], value)
            send[:, lanes + t * LANES : lanes + (t + 1) * LANES] = repeat_rows(value, subs).astype(BF16)

    def prolong_maps(tiles, maps, base):
        kind = maps[base + (1 + tail) * own : base + (2 + tail) * own, :LANES].astype(F32)
        return prolong(tiles, maps[base : base + own, :], maps[base + own : base + (1 + tail) * own, :], kind)

    def combine(got, res_own, gives, members, sol, send, third, spread, token):
        token[...] = jnp.zeros((ROWS, LANES), F32)
        values = res_own[...] + dot(gives[:own, :], got[:, :lanes])
        spread[...] = values
        send[:, :lanes] = dot(gives[own:, :own], values.astype(BF16)).astype(BF16)
        total = jnp.sum(got[:, lanes : lanes + block].astype(F32).reshape(subs, ROWS, block), axis=0)
        for t in range(main):
            columns = slice(t * LANES, (t + 1) * LANES)
            value = tile(total, t) + members[:, columns] * sol[:, columns]
            send[:, lanes + t * LANES : lanes + (t + 1) * LANES] = repeat_rows(value, subs).astype(BF16)
        third[...] = got[:, lanes + block :]

    def end(got, res_own, first, gives, maps, out):
        applied = res_own[...] + dot(gives[...], got[:, :lanes])
        applied += prolong_maps(got[:, lanes:], maps, at_own)
        sums = got[:, lanes + aux * LANES :].astype(F32).reshape(subs, ROWS, LANES)
        sums = jnp.sum(sums, axis=0)
        scale = sums[cl_dev : cl_dev + 1] / (sums[cl_dev + 1 : cl_dev + 2] + EPSILON)
        for k in range(comps):
            out[k] = first[k] - (scale * tile(applied, k)).T

    return dict(locals())


def place_of():
    index = lax.axis_index("group")
    return index % 2, index // 2


def pass_round(kept, given):
    turns = kept.shape[0]
    groups = 2 * turns
    other = lax.ppermute(given, "group", [(i, i ^ 1) for i in range(groups)])
    pieces = [kept[0], other[0]]
    for step in range(1, turns):
        piece = jnp.stack([kept[step], other[step]])
        pieces.append(lax.ppermute(piece, "group", [(i, (i - 2 * step) % groups) for i in range(groups)]))
    return pieces


def body(residual_in, local_inverse, coarse_inverse, cluster_of, margin_peer, margin_row):
    rhs, comps, own = residual_in.shape
    over = margin_row.shape[0]
    subs = lax.axis_size("sub")
    groups = lax.axis_size("group")
    cl_dev = coarse_inverse.shape[0] // comps
    width = local_inverse.shape[1]
    m = make(rhs, comps, own, over, subs, groups, cl_dev)
    slots, lanes, block, main, tail = m["slots"], m["lanes"], m["block"], m["main"], m["tail"]
    share = m["share"]
    each = main * ROWS
    inverse = local_inverse.reshape(comps, 2, own, width)
    residual = residual_in.transpose(1, 0, 2)
    cluster, peer, row = [values.reshape(1, -1) for values in (cluster_of, margin_peer, margin_row)]
    hbm = pl.BlockSpec(memory_space=pltpu.HBM)
    here = pl.BlockSpec(memory_space=pltpu.VMEM)
    vmem = pltpu.VMEM
    half_cost = dict(flops=rhs * width * width, moved=width * width)
    mark = ((ROWS, LANES), F32)
    half_scratch = [
        vmem((rhs, lanes), BF16),
        vmem((comps, own, width), BF16),
        pltpu.SemaphoreType.DMA((comps,)),
    ]

    def swap(send):
        return exchange(send.reshape(subs, ROWS, send.shape[1]), "sub").reshape(send.shape)

    def coarse_parts(matrix, got, rows, inner, after=()):
        parts = kernel_call(
            functools.partial(m["coarse"], lanes, rows),
            [((groups, rows, LANES), BF16)],
            matrix,
            got,
            *inner,
            after=after,
        )[0]
        return exchange(parts, "group")

    def solve(got, part, *extra):
        return kernel_call(
            m["solve"],
            [((rhs, width), F32)],
            got,
            part,
            maps,
            inverse,
            *extra,
            in_specs=[here, here, here, hbm] + [here] * len(extra),
            scratch_shapes=half_scratch,
            limit=48,
            **half_cost,
        )[0]

    with jax.named_scope("begin"):
        send, token = kernel_call(
            m["begin"],
            [((slots, block), BF16), mark],
            residual,
            cluster,
            peer,
            row,
            in_specs=[hbm] * 4,
            limit=60,
            scratch_shapes=[
                vmem((comps, rhs, own), F32),
                vmem((1, own), jnp.int32),
                vmem((1, over), jnp.int32),
                vmem((1, over), jnp.int32),
                vmem((own, lanes), BF16),
                pltpu.SemaphoreType.DMA((4,)),
            ],
        )
    with jax.named_scope("maps"):
        field16, maps = kernel_call(
            m["keep_maps"],
            [((own, lanes), BF16), ((m["map_rows"], slots), BF16)],
            residual,
            cluster,
            peer,
            after=[token],
        )
    with jax.named_scope("regroup"):
        member = lax.axis_index("sub") % RING
        place = jnp.stack(place_of() + (member,)).astype(jnp.int32).reshape(1, 3)
        columns = main * slots
        kept, given = kernel_call(
            m["prepare"],
            [((groups // 2, each, columns), BF16)] * 2,
            place,
            coarse_inverse,
            after=[token],
            in_specs=[pl.BlockSpec(memory_space=pltpu.SMEM), here],
            scratch_shapes=[vmem((groups, each, columns), BF16)],
            flops=2 * groups * each * columns * columns,
        )
    with jax.named_scope("answer"):
        got = swap(send)
        send, token = kernel_call(
            m["answer"], [((slots, lanes + block), BF16), mark], got, field16, cluster
        )
        gives, gives_late, members = kernel_call(
            m["keep_answer"],
            [((own + slots, slots), BF16), ((own, slots), BF16), ((ROWS, block), F32)],
            got,
            after=[token],
        )
    with jax.named_scope("own_half_first"):
        part, half_token = kernel_call(
            m["half"],
            [((rhs, width), F32), mark],
            residual,
            inverse,
            after=[token],
            in_specs=[here, hbm],
            scratch_shapes=half_scratch,
            **half_cost,
        )
    with jax.named_scope("regroup"):
        pieces = pass_round(kept, given)
        matrix, matrix_late = kernel_call(
            m["gather"],
            [((groups, each, columns), BF16)] * 2,
            place,
            *pieces,
            after=[half_token],
            in_specs=[pl.BlockSpec(memory_space=pltpu.SMEM)] + [here] * len(pieces),
        )
    got = swap(send)

    with jax.named_scope("coarse_first"):
        parts = coarse_parts(matrix, got, each, [], [half_token, members])
    with jax.named_scope("solve_first"):
        total = solve(got, part)
    with jax.named_scope("return_first"):
        send, res_own, over_maps, sol, token = kernel_call(
            m["finish_first"],
            [
                ((slots, lanes + block + share), BF16),
                ((own, lanes), F32),
                (((2 + tail) * own, slots), BF16),
                ((ROWS, block), F32),
                mark,
            ],
            got,
            total,
            parts,
            maps,
            scratch_shapes=[vmem((own, lanes), BF16), vmem((over, lanes), BF16)],
        )
        got = swap(send)
    with jax.named_scope("combine"):
        send, third, spread, token = kernel_call(
            m["combine"],
            [((slots, lanes + block), BF16), ((slots, share), BF16), ((own, lanes), F32), mark],
            got,
            res_own,
            gives,
            members,
            sol,
        )
    with jax.named_scope("own_half_second"):
        pieces_x = [third]
        for step in range(1, RING):
            turn = [(i, i // RING * RING + (i - step) % RING) for i in range(subs)]
            pieces_x.append(lax.ppermute(third, "sub", turn))
        first, inner, part, over_add = kernel_call(
            m["half_first"],
            [((comps, rhs, own), F32), ((2, LANES), F32), ((rhs, width), F32), ((over, lanes), F32)],
            place,
            spread,
            maps,
            over_maps,
            residual,
            inverse,
            *pieces_x,
            after=[token],
            in_specs=[pl.BlockSpec(memory_space=pltpu.SMEM)] + [here] * 4 + [hbm] + [here] * RING,
            scratch_shapes=half_scratch + [vmem((slots, block), BF16)],
            limit=48,
            **half_cost,
        )
    got = swap(send)
    with jax.named_scope("coarse_second"):
        parts = coarse_parts(matrix_late, got, each + 16, [inner])
    with jax.named_scope("solve_second"):
        total = solve(got, part, over_add)
    with jax.named_scope("return_second"):
        send, res_own = kernel_call(
            m["finish_second"],
            [((slots, lanes + block), BF16), ((own, lanes), F32)],
            total,
            parts,
            maps,
            scratch_shapes=[vmem((over, lanes), BF16)],
        )
        got = swap(send)
    with jax.named_scope("end"):
        second = kernel_call(m["end"], [((comps, rhs, own), F32)], got, res_own, first, gives_late, maps)[0]
    return first.transpose(1, 0, 2), second.transpose(1, 0, 2)


def solution(mesh):
    placed = (
        P(None, None, ("group", "sub")),
        P(("group", "sub"), None, None),
        P(("group", "sub"), None),
        P(("group", "sub")),
        P(("group", "sub"), None),
        P(("group", "sub")),
    )
    return jax.shard_map(
        body,
        mesh=mesh,
        in_specs=placed,
        out_specs=(P(None, None, ("group", "sub")), P(None, None, ("group", "sub"))),
        check_vma=False,
    )
```

```python
import functools

import jax
import jax.numpy as jnp
from jax import lax
from jax.experimental import pallas as pl
from jax.experimental.pallas import tpu as pltpu
from jax.sharding import PartitionSpec as P

EPSILON = 1e-06
F32 = jnp.float32
BF16 = jnp.bfloat16
LANES = 128
ROWS = 8
RING = 4


def dot(left, right):
    return jnp.dot(left, right, preferred_element_type=F32)


def exchange(values, axis):
    return lax.all_to_all(values, axis, split_axis=0, concat_axis=0, tiled=True)


def tile(values, index):
    return values[:, index * LANES : (index + 1) * LANES]


def iota(shape, axis):
    return lax.broadcasted_iota(jnp.int32, shape, axis)


def over_rows(values, subs):
    cube = values.reshape(subs, ROWS, LANES)
    return jnp.broadcast_to(jnp.sum(cube, axis=1, keepdims=True), cube.shape).reshape(subs * ROWS, LANES)


def one_row(values, row, subs):
    cube = values.reshape(subs, ROWS, LANES)
    return jnp.broadcast_to(cube[:, row : row + 1, :], cube.shape).reshape(subs * ROWS, LANES)


def repeat_rows(values, subs):
    return jnp.broadcast_to(values[None], (subs,) + values.shape).reshape(subs * ROWS, values.shape[1])


def kernel_call(body, outs, *args, flops=0, moved=0, limit=48, after=(), in_specs=None, **kw):
    count = len(after)
    specs = in_specs or [pl.BlockSpec(memory_space=pltpu.VMEM)] * len(args)
    return pl.pallas_call(
        lambda *refs: body(*refs[count:]),
        out_shape=[jax.ShapeDtypeStruct(shape, dtype) for shape, dtype in outs],
        in_specs=[pl.BlockSpec(memory_space=pl.ANY)] * count + list(specs),
        compiler_params=pltpu.CompilerParams(vmem_limit_bytes=limit * 1024 * 1024),
        cost_estimate=pl.CostEstimate(flops=flops, bytes_accessed=moved, transcendentals=0),
        **kw,
    )(*after, *args)


def make(rhs, comps, own, over, subs, groups, cl_dev):
    tail = ROWS - cl_dev
    main = comps - tail
    slots = subs * ROWS
    lanes = comps * LANES
    block = main * LANES
    share = -(-main // RING) * LANES
    aux = main - 1
    at_take, at_own, at_tail = 0, over, over + own
    at_kind = at_tail + tail * own
    at_rows = at_kind + own
    map_rows = at_rows + slots

    def pack(sums, extra, ref, offset):
        inner = iota((slots, LANES), 0) % ROWS
        for t in range(main):
            value = tile(sums, t)
            if t < cl_dev:
                for j in range(tail):
                    value = jnp.where(inner == cl_dev + j, one_row(tile(sums, main + j), t, subs), value)
            elif extra is not None:
                value = jnp.where(inner == cl_dev, extra, value)
            ref[:, offset + t * LANES : offset + (t + 1) * LANES] = value.astype(BF16)

    def prolong(tiles, own8t, own_tail, own_kind):
        head = dot(own8t, tiles)
        picked = dot(own_tail, tiles[:, : cl_dev * LANES])
        parts = [head]
        for j in range(tail):
            rows = picked[j * own : (j + 1) * own]
            value = jnp.zeros((own, LANES), F32)
            for t in range(cl_dev):
                value = jnp.where(own_kind == t, tile(rows, t), value)
            parts.append(value)
        return jnp.concatenate(parts, axis=1)

    def places(cl, peer):
        number = cl[...]
        holder = ((number.astype(F32) + 0.5) * (1.0 / cl_dev)).astype(jnp.int32)
        kind = number - holder * cl_dev
        rows = iota((slots, own), 0)
        hot = (rows == holder * ROWS + kind).astype(F32)
        peers = jnp.broadcast_to(peer[...].astype(F32), (over, over))
        same = (peers == peers.T) & (iota((over, over), 0) < iota((over, over), 1))
        rank = jnp.sum(same.astype(F32), axis=0, keepdims=True).astype(jnp.int32)
        dest = peer[...] * ROWS + rank
        hot_dest = (iota((slots, over), 0) == dest).astype(F32)
        return rows, holder, kind, hot, hot_dest

    def begin(res_hbm, cl_hbm, peer_hbm, row_hbm, send, token, res, cl, peer, row, field16, sems):
        token[...] = jnp.zeros((ROWS, LANES), F32)
        third = comps // 3
        pairs = [(peer_hbm, peer), (row_hbm, row), (cl_hbm, cl)]
        pairs += [(res_hbm.at[pl.ds(j * third, third)], res.at[pl.ds(j * third, third)]) for j in range(3)]
        copies = [pltpu.make_async_copy(src, dst, sems.at[i]) for i, (src, dst) in enumerate(pairs)]
        for copy in copies:
            copy.start()
        for copy in copies[:3]:
            copy.wait()
        rows, holder, kind, hot, hot_dest = places(cl, peer)
        inner = rows % ROWS
        lane = iota((slots, LANES), 1)
        wanted = jnp.sum(hot_dest * (row[...] + 1).astype(F32), axis=1, keepdims=True)
        counts = jnp.sum(hot, axis=1, keepdims=True)
        extra = jnp.where(lane == inner, wanted, 0.0) + jnp.where(lane == inner + ROWS, counts, 0.0)
        for k in range(comps):
            if k % third == 0:
                copies[3 + k // third].wait()
            field16[:, k * LANES : (k + 1) * LANES] = res[k].T.astype(BF16)
        pack(dot(hot.astype(BF16), field16[...]), over_rows(extra, subs), send, 0)

    def keep_maps(res, cl, peer, field16, maps):
        for k in range(comps):
            field16[:, k * LANES : (k + 1) * LANES] = res[k].T.astype(BF16)
        rows, holder, kind, hot, hot_dest = places(cl, peer)
        maps[at_take : at_take + over, :] = hot_dest.T.astype(BF16)
        cluster_maps(holder, kind, maps, at_own)
        maps[at_rows : at_rows + slots, :over] = hot_dest.astype(BF16)
        maps[at_rows : at_rows + slots, over : over + own] = hot.astype(BF16)

    def asking(got):
        lane = iota((slots, LANES), 1)
        inner = iota((slots, LANES), 0) % ROWS
        asked = one_row(tile(got, aux).astype(F32), cl_dev, subs)
        asked = jnp.sum(jnp.where(lane == inner, asked, 0.0), axis=1, keepdims=True) - 1.0
        hot = (iota((slots, own), 1).astype(F32) == asked).astype(F32)
        return lane, inner, hot

    def answer(got, field16, cl, send, token):
        token[...] = jnp.zeros((ROWS, LANES), F32)
        total = jnp.sum(got[...].astype(F32).reshape(subs, ROWS, block), axis=0)
        lane, inner, hot = asking(got)
        send[:, :lanes] = dot(hot.astype(BF16), field16[...]).astype(BF16)
        ids = jnp.sum(hot * cl[...].astype(F32), axis=1, keepdims=True)
        ids = over_rows(jnp.where(lane == inner, ids, 0.0), subs)
        for t in range(main):
            value = repeat_rows(tile(total, t), subs)
            if t >= cl_dev:
                value = jnp.where(inner == cl_dev, ids, value)
            send[:, lanes + t * LANES : lanes + (t + 1) * LANES] = value.astype(BF16)

    def keep_answer(got, gives, gives_late, members):
        lane, inner, hot = asking(got)
        gives_late[...] = hot.T.astype(BF16)
        gives[:own, :] = hot.T.astype(BF16)
        gives[own:, :own] = hot.astype(BF16)
        gives[own:, own:] = jnp.zeros((slots, slots - own), BF16)
        total = jnp.sum(tile(got, aux).astype(F32).reshape(subs, ROWS, LANES), axis=0)
        small = iota((ROWS, LANES), 0)
        small_lane = iota((ROWS, LANES), 1)
        numbers = [
            jnp.sum(jnp.where((small_lane == ROWS + c) & (small == cl_dev), total, 0.0), axis=(0, 1), keepdims=True)
            for c in range(cl_dev)
        ]
        base = jnp.zeros((ROWS, LANES), F32)
        for c in range(cl_dev):
            base = jnp.where(small == c, numbers[c], base)
        for t in range(main):
            count = jnp.where(small < cl_dev, base, numbers[t]) if t < cl_dev else base
            members[:, t * LANES : (t + 1) * LANES] = count

    def prepare(place, rows, kept, given, lined):
        cl_rows = cl_dev * comps
        grp_rows = cl_rows * subs
        each = main * ROWS
        window = main * slots
        turns = groups // 2
        at = iota((each, cl_rows), 0)
        t, i = at // ROWS, at % ROWS
        source = jnp.where(i < cl_dev, i * comps + t, t * comps + main + i - cl_dev)
        source = jnp.where((i < cl_dev) | (t < cl_dev), source, -1)
        pick = (source == iota((each, cl_rows), 1)).astype(F32).astype(BF16)
        for g in range(groups):
            start = g * grp_rows // LANES * LANES
            values = dot(pick, rows[:, start : start + window])
            shift = g * grp_rows - start
            if shift:
                values = pltpu.roll(values, window - shift, 1)
            lined[g] = values.astype(BF16)
        turned = []
        for side in range(2):
            parts = []
            for step in range(turns):
                turn = place[0, 1] - step
                turn = jnp.where(turn < 0, turn + turns, turn)
                core = place[0, 0] if side == 0 else 1 - place[0, 0]
                parts.append(lined[2 * turn + core])
            turned.append(jnp.concatenate(parts, axis=0))
        lane = iota((window, slots), 1)
        row = iota((window, slots), 0)
        holder, i = lane // ROWS, lane % ROWS
        for t in range(main):
            if t < cl_dev:
                source = holder * cl_rows + jnp.where(i < cl_dev, i * comps + t, t * comps + main + i - cl_dev)
            else:
                source = jnp.where(i < cl_dev, holder * cl_rows + i * comps + t, -1)
            moved = (source == row).astype(F32).astype(BF16)
            for values, out in zip(turned, (kept, given)):
                value = dot(values, moved).astype(BF16)
                for step in range(turns):
                    out[step, :, t * slots : (t + 1) * slots] = value[step * each : (step + 1) * each]

    def gather(place, own_piece, other_piece, *refs):
        pieces, outs = refs[:-2], refs[-2:]
        turns = len(pieces) + 1
        for step in range(turns):
            turn = place[0, 1] + step
            turn = jnp.where(turn >= turns, turn - turns, turn)
            for side in range(2):
                core = place[0, 0] if side == 0 else 1 - place[0, 0]
                value = pieces[step - 1][side] if step else (own_piece, other_piece)[side][...]
                for out in outs:
                    out[2 * turn + core] = value

    def coarse(offset, rows, matrix, got, *refs):
        out = refs[-1]
        each = main * ROWS
        total = jnp.zeros((groups * each, LANES), F32)
        for t in range(main):
            columns = matrix[:, :, t * slots : (t + 1) * slots].reshape(groups * each, slots)
            total += dot(columns, got[:, offset + t * LANES : offset + (t + 1) * LANES])
        for g in range(groups):
            out[g, :each, :] = total[g * each : (g + 1) * each].astype(BF16)
        if rows > each:
            inner = refs[0][...]
            high = inner.astype(BF16).astype(F32)
            last = jnp.concatenate([high, inner - high, jnp.zeros((rows - each - 4, LANES), F32)], axis=0)
            for g in range(groups):
                out[g, each:, :] = last.astype(BF16)

    def group_total(got):
        total = jnp.sum(got[...].astype(F32), axis=0)
        return total, [total[t * ROWS : (t + 1) * ROWS] for t in range(main)]

    def loads(inverse, which, buffer, sems):
        copies = [pltpu.make_async_copy(inverse.at[k, which], buffer.at[k], sems.at[k]) for k in range(comps)]
        for copy in copies:
            copy.start()
        return copies

    def product(copies, turned, buffer, part, out):
        third = comps // 3
        for step in range(3):
            for copy in copies[step * third : (step + 1) * third]:
                copy.wait()
            rows = buffer[step * third : (step + 1) * third].reshape(third * own, out.shape[1])
            value = dot(turned[:, step * third * LANES : (step + 1) * third * LANES], rows)
            if step:
                out[...] += value
            elif part is None:
                out[...] = value
            else:
                out[...] = part[...] + value

    def half(res, inverse, out, token, turned, buffer, sems):
        token[...] = jnp.zeros((ROWS, LANES), F32)
        copies = loads(inverse, 0, buffer, sems)
        for k in range(comps):
            turned[:, k * LANES : (k + 1) * LANES] = res[k].astype(BF16)
        product(copies, turned, buffer, None, out)

    def half_first(place, spread, maps, over_maps, res, inverse, *refs):
        pieces, refs = refs[:RING], refs[RING:]
        first_out, inner, both, turned, buffer, sems, tiles = refs
        out = both.at[:, : (own + over) * comps]
        copies = loads(inverse, 0, buffer, sems)
        for step, piece in enumerate(pieces):
            member = place[0, 2] + step
            member = jnp.where(member >= RING, member - RING, member)

            @pl.when(member * share < block)
            def _(piece=piece, member=member):
                tiles[:, pl.ds(pl.multiple_of(member * share, LANES), share)] = piece[...]

        everything = tiles[...]
        values = spread[...] + prolong_maps(everything, maps, at_own)
        both[:, (own + over) * comps :] = prolong_maps(everything, over_maps, 0)
        rf = jnp.zeros((rhs, own), F32)
        ff = jnp.zeros((rhs, own), F32)
        for k in range(comps):
            flipped = tile(values, k).T
            first_out[k] = flipped
            turned[:, k * LANES : (k + 1) * LANES] = flipped.astype(BF16)
            rf += res[k] * flipped
            ff += flipped * flipped
        inner[0:1, :] = jnp.sum(rf.T, axis=0, keepdims=True)
        inner[1:2, :] = jnp.sum(ff.T, axis=0, keepdims=True)
        product(copies, turned, buffer, None, out)

    def solve(got, part, maps, inverse, *refs):
        out, turned, buffer, sems = refs
        size = out.shape[1]
        copies = loads(inverse, 1, buffer, sems)
        arrived = dot(maps[at_take : at_take + over, :], got[:, :lanes])
        if part.shape[1] > size:
            arrived += part[:, size:]
        for k in range(comps):
            turned[:, k * LANES : (k + 1) * LANES] = tile(arrived, k).T.astype(BF16)
        product(copies, turned, buffer, part.at[:, :size], out)

    def finish_first(got, total, parts, maps, send, res_own, over_maps, sol, token, own16, over16):
        token[...] = jnp.zeros((ROWS, LANES), F32)
        cams = own + over
        for k in range(comps):
            flipped = total[:, k * cams : (k + 1) * cams].T
            res_own[:, k * LANES : (k + 1) * LANES] = flipped[:own]
            flipped = flipped.astype(BF16)
            own16[:, k * LANES : (k + 1) * LANES] = flipped[:own]
            over16[:, k * LANES : (k + 1) * LANES] = flipped[own:]
        rows = maps[at_rows : at_rows + slots, :]
        take_t, own8 = rows[:, :over], rows[:, over : over + own]
        send[:, :lanes] = dot(take_t, over16[...]).astype(BF16)
        holder, kind = margin_places(got, take_t)
        cluster_maps(holder, kind, over_maps, 0)
        over8 = (iota((slots, over), 0) == holder * ROWS + kind).astype(F32).astype(BF16)
        pack(dot(own8, own16[...]) + dot(over8, over16[...]), None, send, lanes)
        _, tiles = group_total(parts)
        each_share = share // LANES
        for t in range(main):
            sol[:, t * LANES : (t + 1) * LANES] = tiles[t]
        member = iota((slots, LANES), 0) // ROWS % RING
        for j in range(each_share):
            value = jnp.zeros((slots, LANES), F32)
            for q in range(RING):
                if q * each_share + j < main:
                    value = jnp.where(member == q, repeat_rows(tiles[q * each_share + j], subs), value)
            at = lanes + block + j * LANES
            send[:, at : at + LANES] = value.astype(BF16)

    def margin_places(got, take_t):
        lane = iota((slots, LANES), 1)
        inner = iota((slots, LANES), 0) % ROWS
        ids = one_row(got[:, lanes + aux * LANES : lanes + (aux + 1) * LANES].astype(F32), cl_dev, subs)
        ids = jnp.sum(jnp.where(lane == inner, ids, 0.0), axis=1, keepdims=True)
        number = jnp.sum(take_t.astype(F32) * ids, axis=0, keepdims=True)
        holder = ((number + 0.5) * (1.0 / cl_dev)).astype(jnp.int32)
        return holder, number.astype(jnp.int32) - holder * cl_dev

    def cluster_maps(holder, kind, maps, base):
        rows = iota((slots, own), 0)
        hot = (rows == holder * ROWS + kind).astype(F32)
        maps[base : base + own, :] = hot.T.astype(BF16)
        for j in range(tail):
            hot_j = (rows == holder * ROWS + (cl_dev + j)).astype(F32)
            maps[base + (1 + j) * own : base + (2 + j) * own, :] = hot_j.T.astype(BF16)
        at = base + (1 + tail) * own
        maps[at : at + own, :] = jnp.broadcast_to(kind.astype(F32), (slots, own)).T.astype(BF16)

    def finish_second(total, parts, maps, send, res_own, over16):
        cams = own + over
        for k in range(comps):
            flipped = total[:, k * cams : (k + 1) * cams].T
            res_own[:, k * LANES : (k + 1) * LANES] = flipped[:own]
            over16[:, k * LANES : (k + 1) * LANES] = flipped[own:].astype(BF16)
        send[:, :lanes] = dot(maps[at_rows : at_rows + slots, :over], over16[...]).astype(BF16)
        summed, tiles = group_total(parts)
        each = main * ROWS
        inner = summed[each : each + 2] + summed[each + 2 : each + 4]
        low = inner - inner.astype(BF16).astype(F32)
        rest = low[0:1] - inner[0:1] / (inner[1:2] + EPSILON) * low[1:2]
        small = iota((ROWS, LANES), 0)
        for t in range(main):
            value = tiles[t]
            if t == aux:
                value = jnp.where(small == cl_dev, inner[0:1], value)
                value = jnp.where(small == cl_dev + 1, inner[1:2], value)
                value = jnp.where(small == cl_dev + 2, rest, value)
            send[:, lanes + t * LANES : lanes + (t + 1) * LANES] = repeat_rows(value, subs).astype(BF16)

    def prolong_maps(tiles, maps, base):
        kind = maps[base + (1 + tail) * own : base + (2 + tail) * own, :LANES].astype(F32)
        return prolong(tiles, maps[base : base + own, :], maps[base + own : base + (1 + tail) * own, :], kind)

    def combine(got, res_own, gives, members, sol, send, third, spread, token):
        token[...] = jnp.zeros((ROWS, LANES), F32)
        values = res_own[...] + dot(gives[:own, :], got[:, :lanes])
        spread[...] = values
        send[:, :lanes] = dot(gives[own:, :own], values.astype(BF16)).astype(BF16)
        total = jnp.sum(got[:, lanes : lanes + block].astype(F32).reshape(subs, ROWS, block), axis=0)
        for t in range(main):
            columns = slice(t * LANES, (t + 1) * LANES)
            value = tile(total, t) + members[:, columns] * sol[:, columns]
            send[:, lanes + t * LANES : lanes + (t + 1) * LANES] = repeat_rows(value, subs).astype(BF16)
        third[...] = got[:, lanes + block :]

    def end(got, res_own, first, gives, maps, out):
        applied = res_own[...] + dot(gives[...], got[:, :lanes])
        applied += prolong_maps(got[:, lanes:], maps, at_own)
        sums = got[:, lanes + aux * LANES :].astype(F32).reshape(subs, ROWS, LANES)
        sums = jnp.sum(sums, axis=0)
        scale = (sums[cl_dev : cl_dev + 1] + sums[cl_dev + 2 : cl_dev + 3]) / (sums[cl_dev + 1 : cl_dev + 2] + EPSILON)
        for k in range(comps):
            out[k] = first[k] - (scale * tile(applied, k)).T

    return dict(locals())


def place_of():
    index = lax.axis_index("group")
    return index % 2, index // 2


def pass_round(kept, given):
    turns = kept.shape[0]
    groups = 2 * turns
    other = lax.ppermute(given, "group", [(i, i ^ 1) for i in range(groups)])
    pieces = [kept[0], other[0]]
    for step in range(1, turns):
        piece = jnp.stack([kept[step], other[step]])
        pieces.append(lax.ppermute(piece, "group", [(i, (i - 2 * step) % groups) for i in range(groups)]))
    return pieces


def body(residual_in, local_inverse, coarse_inverse, cluster_of, margin_peer, margin_row):
    rhs, comps, own = residual_in.shape
    over = margin_row.shape[0]
    subs = lax.axis_size("sub")
    groups = lax.axis_size("group")
    cl_dev = coarse_inverse.shape[0] // comps
    width = local_inverse.shape[1]
    m = make(rhs, comps, own, over, subs, groups, cl_dev)
    slots, lanes, block, main, tail = m["slots"], m["lanes"], m["block"], m["main"], m["tail"]
    share = m["share"]
    each = main * ROWS
    inverse = local_inverse.reshape(comps, 2, own, width)
    residual = residual_in.transpose(1, 0, 2)
    cluster, peer, row = [values.reshape(1, -1) for values in (cluster_of, margin_peer, margin_row)]
    hbm = pl.BlockSpec(memory_space=pltpu.HBM)
    here = pl.BlockSpec(memory_space=pltpu.VMEM)
    vmem = pltpu.VMEM
    half_cost = dict(flops=rhs * width * width, moved=width * width)
    mark = ((ROWS, LANES), F32)
    half_scratch = [
        vmem((rhs, lanes), BF16),
        vmem((comps, own, width), BF16),
        pltpu.SemaphoreType.DMA((comps,)),
    ]

    def swap(send):
        return exchange(send.reshape(subs, ROWS, send.shape[1]), "sub").reshape(send.shape)

    def coarse_parts(matrix, got, rows, inner, after=()):
        parts = kernel_call(
            functools.partial(m["coarse"], lanes, rows),
            [((groups, rows, LANES), BF16)],
            matrix,
            got,
            *inner,
            after=after,
        )[0]
        return exchange(parts, "group")

    def solve(got, part):
        return kernel_call(
            m["solve"],
            [((rhs, width), F32)],
            got,
            part,
            maps,
            inverse,
            in_specs=[here, here, here, hbm],
            scratch_shapes=half_scratch,
            limit=48,
            **half_cost,
        )[0]

    with jax.named_scope("begin"):
        send, token = kernel_call(
            m["begin"],
            [((slots, block), BF16), mark],
            residual,
            cluster,
            peer,
            row,
            in_specs=[hbm] * 4,
            limit=60,
            scratch_shapes=[
                vmem((comps, rhs, own), F32),
                vmem((1, own), jnp.int32),
                vmem((1, over), jnp.int32),
                vmem((1, over), jnp.int32),
                vmem((own, lanes), BF16),
                pltpu.SemaphoreType.DMA((6,)),
            ],
        )
    with jax.named_scope("maps"):
        field16, maps = kernel_call(
            m["keep_maps"],
            [((own, lanes), BF16), ((m["map_rows"], slots), BF16)],
            residual,
            cluster,
            peer,
            after=[token],
        )
    with jax.named_scope("regroup"):
        member = lax.axis_index("sub") % RING
        place = jnp.stack(place_of() + (member,)).astype(jnp.int32).reshape(1, 3)
        columns = main * slots
        kept, given = kernel_call(
            m["prepare"],
            [((groups // 2, each, columns), BF16)] * 2,
            place,
            coarse_inverse,
            after=[token],
            in_specs=[pl.BlockSpec(memory_space=pltpu.SMEM), here],
            scratch_shapes=[vmem((groups, each, columns), BF16)],
            flops=2 * groups * each * columns * columns,
        )
    with jax.named_scope("answer"):
        got = swap(send)
        send, token = kernel_call(
            m["answer"], [((slots, lanes + block), BF16), mark], got, field16, cluster
        )
        gives, gives_late, members = kernel_call(
            m["keep_answer"],
            [((own + slots, slots), BF16), ((own, slots), BF16), ((ROWS, block), F32)],
            got,
            after=[token],
        )
    with jax.named_scope("own_half_first"):
        part, half_token = kernel_call(
            m["half"],
            [((rhs, width), F32), mark],
            residual,
            inverse,
            after=[token],
            in_specs=[here, hbm],
            scratch_shapes=half_scratch,
            **half_cost,
        )
    with jax.named_scope("regroup"):
        pieces = pass_round(kept, given)
        matrix, matrix_late = kernel_call(
            m["gather"],
            [((groups, each, columns), BF16)] * 2,
            place,
            *pieces,
            after=[half_token],
            in_specs=[pl.BlockSpec(memory_space=pltpu.SMEM)] + [here] * len(pieces),
        )
    got = swap(send)

    with jax.named_scope("coarse_first"):
        parts = coarse_parts(matrix, got, each, [], [half_token, members])
    with jax.named_scope("solve_first"):
        total = solve(got, part)
    with jax.named_scope("return_first"):
        send, res_own, over_maps, sol, token = kernel_call(
            m["finish_first"],
            [
                ((slots, lanes + block + share), BF16),
                ((own, lanes), F32),
                (((2 + tail) * own, slots), BF16),
                ((ROWS, block), F32),
                mark,
            ],
            got,
            total,
            parts,
            maps,
            scratch_shapes=[vmem((own, lanes), BF16), vmem((over, lanes), BF16)],
        )
        got = swap(send)
    with jax.named_scope("combine"):
        send, third, spread, token = kernel_call(
            m["combine"],
            [((slots, lanes + block), BF16), ((slots, share), BF16), ((own, lanes), F32), mark],
            got,
            res_own,
            gives,
            members,
            sol,
        )
    with jax.named_scope("own_half_second"):
        pieces_x = [third]
        for step in range(1, RING):
            turn = [(i, i // RING * RING + (i - step) % RING) for i in range(subs)]
            pieces_x.append(lax.ppermute(third, "sub", turn))
        first, inner, part = kernel_call(
            m["half_first"],
            [((comps, rhs, own), F32), ((2, LANES), F32), ((rhs, width + lanes), F32)],
            place,
            spread,
            maps,
            over_maps,
            residual,
            inverse,
            *pieces_x,
            after=[token],
            in_specs=[pl.BlockSpec(memory_space=pltpu.SMEM)] + [here] * 4 + [hbm] + [here] * RING,
            scratch_shapes=half_scratch + [vmem((slots, block), BF16)],
            limit=48,
            **half_cost,
        )
    got = swap(send)
    with jax.named_scope("coarse_second"):
        parts = coarse_parts(matrix_late, got, each + 16, [inner])
    with jax.named_scope("solve_second"):
        total = solve(got, part)
    with jax.named_scope("return_second"):
        send, res_own = kernel_call(
            m["finish_second"],
            [((slots, lanes + block), BF16), ((own, lanes), F32)],
            total,
            parts,
            maps,
            scratch_shapes=[vmem((over, lanes), BF16)],
        )
        got = swap(send)
    with jax.named_scope("end"):
        second = kernel_call(m["end"], [((comps, rhs, own), F32)], got, res_own, first, gives_late, maps)[0]
    return first.transpose(1, 0, 2), second.transpose(1, 0, 2)


def solution(mesh):
    placed = (
        P(None, None, ("group", "sub")),
        P(("group", "sub"), None, None),
        P(("group", "sub"), None),
        P(("group", "sub")),
        P(("group", "sub"), None),
        P(("group", "sub")),
    )
    return jax.shard_map(
        body,
        mesh=mesh,
        in_specs=placed,
        out_specs=(P(None, None, ("group", "sub")), P(None, None, ("group", "sub"))),
        check_vma=False,
    )
```

```python
import functools

import jax
import jax.numpy as jnp
from jax import lax
from jax.experimental import pallas as pl
from jax.experimental.pallas import tpu as pltpu
from jax.sharding import PartitionSpec as P

EPSILON = 1e-06
F32 = jnp.float32
BF16 = jnp.bfloat16
LANES = 128
ROWS = 8
RING = 4


def dot(left, right):
    return jnp.dot(left, right, preferred_element_type=F32)


def exchange(values, axis):
    return lax.all_to_all(values, axis, split_axis=0, concat_axis=0, tiled=True)


def tile(values, index):
    return values[:, index * LANES : (index + 1) * LANES]


def iota(shape, axis):
    return lax.broadcasted_iota(jnp.int32, shape, axis)


def over_rows(values, subs):
    cube = values.reshape(subs, ROWS, LANES)
    return jnp.broadcast_to(jnp.sum(cube, axis=1, keepdims=True), cube.shape).reshape(subs * ROWS, LANES)


def one_row(values, row, subs):
    cube = values.reshape(subs, ROWS, LANES)
    return jnp.broadcast_to(cube[:, row : row + 1, :], cube.shape).reshape(subs * ROWS, LANES)


def repeat_rows(values, subs):
    return jnp.broadcast_to(values[None], (subs,) + values.shape).reshape(subs * ROWS, values.shape[1])


def kernel_call(body, outs, *args, flops=0, moved=0, limit=48, after=(), in_specs=None, **kw):
    count = len(after)
    specs = in_specs or [pl.BlockSpec(memory_space=pltpu.VMEM)] * len(args)
    return pl.pallas_call(
        lambda *refs: body(*refs[count:]),
        out_shape=[jax.ShapeDtypeStruct(shape, dtype) for shape, dtype in outs],
        in_specs=[pl.BlockSpec(memory_space=pl.ANY)] * count + list(specs),
        compiler_params=pltpu.CompilerParams(vmem_limit_bytes=limit * 1024 * 1024),
        cost_estimate=pl.CostEstimate(flops=flops, bytes_accessed=moved, transcendentals=0),
        **kw,
    )(*after, *args)


def make(rhs, comps, own, over, subs, groups, cl_dev):
    tail = ROWS - cl_dev
    main = comps - tail
    slots = subs * ROWS
    lanes = comps * LANES
    block = main * LANES
    share = -(-main // RING) * LANES
    aux = main - 1
    at_take, at_own, at_tail = 0, over, over + own
    at_kind = at_tail + tail * own
    at_rows = at_kind + own
    map_rows = at_rows + slots

    def pack(sums, extra, ref, offset):
        inner = iota((slots, LANES), 0) % ROWS
        for t in range(main):
            value = tile(sums, t)
            if t < cl_dev:
                for j in range(tail):
                    value = jnp.where(inner == cl_dev + j, one_row(tile(sums, main + j), t, subs), value)
            elif extra is not None:
                value = jnp.where(inner == cl_dev, extra, value)
            ref[:, offset + t * LANES : offset + (t + 1) * LANES] = value.astype(BF16)

    def prolong(tiles, own8t, own_tail, own_kind):
        head = dot(own8t, tiles)
        picked = dot(own_tail, tiles[:, : cl_dev * LANES])
        parts = [head]
        for j in range(tail):
            rows = picked[j * own : (j + 1) * own]
            value = jnp.zeros((own, LANES), F32)
            for t in range(cl_dev):
                value = jnp.where(own_kind == t, tile(rows, t), value)
            parts.append(value)
        return jnp.concatenate(parts, axis=1)

    def places(cl, peer):
        number = cl[...]
        holder = ((number.astype(F32) + 0.5) * (1.0 / cl_dev)).astype(jnp.int32)
        kind = number - holder * cl_dev
        rows = iota((slots, own), 0)
        hot = (rows == holder * ROWS + kind).astype(F32)
        peers = jnp.broadcast_to(peer[...].astype(F32), (over, over))
        same = (peers == peers.T) & (iota((over, over), 0) < iota((over, over), 1))
        rank = jnp.sum(same.astype(F32), axis=0, keepdims=True).astype(jnp.int32)
        dest = peer[...] * ROWS + rank
        hot_dest = (iota((slots, over), 0) == dest).astype(F32)
        return rows, holder, kind, hot, hot_dest

    def begin(res_hbm, cl_hbm, peer_hbm, row_hbm, send, token, res, cl, peer, row, field16, sems):
        token[...] = jnp.zeros((ROWS, LANES), F32)
        third = comps // 3
        pairs = [(peer_hbm, peer), (row_hbm, row), (cl_hbm, cl)]
        pairs += [(res_hbm.at[pl.ds(j * third, third)], res.at[pl.ds(j * third, third)]) for j in range(3)]
        copies = [pltpu.make_async_copy(src, dst, sems.at[i]) for i, (src, dst) in enumerate(pairs)]
        for copy in copies:
            copy.start()
        for copy in copies[:3]:
            copy.wait()
        rows, holder, kind, hot, hot_dest = places(cl, peer)
        inner = rows % ROWS
        lane = iota((slots, LANES), 1)
        wanted = jnp.sum(hot_dest * (row[...] + 1).astype(F32), axis=1, keepdims=True)
        counts = jnp.sum(hot, axis=1, keepdims=True)
        extra = jnp.where(lane == inner, wanted, 0.0) + jnp.where(lane == inner + ROWS, counts, 0.0)
        for k in range(comps):
            if k % third == 0:
                copies[3 + k // third].wait()
            field16[:, k * LANES : (k + 1) * LANES] = res[k].T.astype(BF16)
        pack(dot(hot.astype(BF16), field16[...]), over_rows(extra, subs), send, 0)

    def keep_maps(res, cl, peer, field16, maps):
        for k in range(comps):
            field16[:, k * LANES : (k + 1) * LANES] = res[k].T.astype(BF16)
        rows, holder, kind, hot, hot_dest = places(cl, peer)
        maps[at_take : at_take + over, :] = hot_dest.T.astype(BF16)
        cluster_maps(holder, kind, maps, at_own)
        maps[at_rows : at_rows + slots, :over] = hot_dest.astype(BF16)
        maps[at_rows : at_rows + slots, over : over + own] = hot.astype(BF16)

    def asking(got):
        lane = iota((slots, LANES), 1)
        inner = iota((slots, LANES), 0) % ROWS
        asked = one_row(tile(got, aux).astype(F32), cl_dev, subs)
        asked = jnp.sum(jnp.where(lane == inner, asked, 0.0), axis=1, keepdims=True) - 1.0
        hot = (iota((slots, own), 1).astype(F32) == asked).astype(F32)
        return lane, inner, hot

    def answer(got, field16, cl, send, token):
        token[...] = jnp.zeros((ROWS, LANES), F32)
        total = jnp.sum(got[...].astype(F32).reshape(subs, ROWS, block), axis=0)
        lane, inner, hot = asking(got)
        send[:, :lanes] = dot(hot.astype(BF16), field16[...]).astype(BF16)
        ids = jnp.sum(hot * cl[...].astype(F32), axis=1, keepdims=True)
        ids = over_rows(jnp.where(lane == inner, ids, 0.0), subs)
        for t in range(main):
            value = repeat_rows(tile(total, t), subs)
            if t >= cl_dev:
                value = jnp.where(inner == cl_dev, ids, value)
            send[:, lanes + t * LANES : lanes + (t + 1) * LANES] = value.astype(BF16)

    def keep_answer(got, gives, gives_late, members):
        lane, inner, hot = asking(got)
        gives_late[...] = hot.T.astype(BF16)
        gives[:own, :] = hot.T.astype(BF16)
        gives[own:, :own] = hot.astype(BF16)
        gives[own:, own:] = jnp.zeros((slots, slots - own), BF16)
        total = jnp.sum(tile(got, aux).astype(F32).reshape(subs, ROWS, LANES), axis=0)
        small = iota((ROWS, LANES), 0)
        small_lane = iota((ROWS, LANES), 1)
        numbers = [
            jnp.sum(jnp.where((small_lane == ROWS + c) & (small == cl_dev), total, 0.0), axis=(0, 1), keepdims=True)
            for c in range(cl_dev)
        ]
        base = jnp.zeros((ROWS, LANES), F32)
        for c in range(cl_dev):
            base = jnp.where(small == c, numbers[c], base)
        for t in range(main):
            count = jnp.where(small < cl_dev, base, numbers[t]) if t < cl_dev else base
            members[:, t * LANES : (t + 1) * LANES] = count

    def prepare(place, rows, kept, given, lined):
        cl_rows = cl_dev * comps
        grp_rows = cl_rows * subs
        each = main * ROWS
        window = main * slots
        turns = groups // 2
        at = iota((each, cl_rows), 0)
        t, i = at // ROWS, at % ROWS
        source = jnp.where(i < cl_dev, i * comps + t, t * comps + main + i - cl_dev)
        source = jnp.where((i < cl_dev) | (t < cl_dev), source, -1)
        pick = (source == iota((each, cl_rows), 1)).astype(F32).astype(BF16)
        for g in range(groups):
            start = g * grp_rows // LANES * LANES
            values = dot(pick, rows[:, start : start + window])
            shift = g * grp_rows - start
            if shift:
                values = pltpu.roll(values, window - shift, 1)
            lined[g] = values.astype(BF16)
        turned = []
        for side in range(2):
            parts = []
            for step in range(turns):
                turn = place[0, 1] - step
                turn = jnp.where(turn < 0, turn + turns, turn)
                core = place[0, 0] if side == 0 else 1 - place[0, 0]
                parts.append(lined[2 * turn + core])
            turned.append(jnp.concatenate(parts, axis=0))
        lane = iota((window, slots), 1)
        row = iota((window, slots), 0)
        holder, i = lane // ROWS, lane % ROWS
        for t in range(main):
            if t < cl_dev:
                source = holder * cl_rows + jnp.where(i < cl_dev, i * comps + t, t * comps + main + i - cl_dev)
            else:
                source = jnp.where(i < cl_dev, holder * cl_rows + i * comps + t, -1)
            moved = (source == row).astype(F32).astype(BF16)
            for values, out in zip(turned, (kept, given)):
                value = dot(values, moved).astype(BF16)
                for step in range(turns):
                    out[step, :, t * slots : (t + 1) * slots] = value[step * each : (step + 1) * each]

    def gather(place, own_piece, other_piece, *refs):
        pieces, outs = refs[:-2], refs[-2:]
        turns = len(pieces) + 1
        for step in range(turns):
            turn = place[0, 1] + step
            turn = jnp.where(turn >= turns, turn - turns, turn)
            for side in range(2):
                core = place[0, 0] if side == 0 else 1 - place[0, 0]
                value = pieces[step - 1][side] if step else (own_piece, other_piece)[side][...]
                for out in outs:
                    out[2 * turn + core] = value

    def coarse(offset, rows, matrix, got, *refs):
        out = refs[-1]
        each = main * ROWS
        total = jnp.zeros((groups * each, LANES), F32)
        for t in range(main):
            columns = matrix[:, :, t * slots : (t + 1) * slots].reshape(groups * each, slots)
            total += dot(columns, got[:, offset + t * LANES : offset + (t + 1) * LANES])
        for g in range(groups):
            out[g, :each, :] = total[g * each : (g + 1) * each].astype(BF16)
        if rows > each:
            inner = refs[0][...]
            high = inner.astype(BF16).astype(F32)
            last = jnp.concatenate([high, inner - high, jnp.zeros((rows - each - 4, LANES), F32)], axis=0)
            for g in range(groups):
                out[g, each:, :] = last.astype(BF16)

    def group_total(got):
        total = jnp.sum(got[...].astype(F32), axis=0)
        return total, [total[t * ROWS : (t + 1) * ROWS] for t in range(main)]

    def loads(inverse, which, buffer, sems):
        copies = [pltpu.make_async_copy(inverse.at[k, which], buffer.at[k], sems.at[k]) for k in range(comps)]
        for copy in copies:
            copy.start()
        return copies

    def product(copies, turned, buffer, part, out):
        third = comps // 3
        for step in range(3):
            for copy in copies[step * third : (step + 1) * third]:
                copy.wait()
            rows = buffer[step * third : (step + 1) * third].reshape(third * own, out.shape[1])
            value = dot(turned[:, step * third * LANES : (step + 1) * third * LANES], rows)
            if step:
                out[...] += value
            elif part is None:
                out[...] = value
            else:
                out[...] = part[...] + value

    def half(res, inverse, far, token, turned, buffer, sems, out, far_sem):
        token[...] = jnp.zeros((ROWS, LANES), F32)
        copies = loads(inverse, 0, buffer, sems)
        for k in range(comps):
            turned[:, k * LANES : (k + 1) * LANES] = res[k].astype(BF16)
        product(copies, turned, buffer, None, out)
        put = pltpu.make_async_copy(out, far.at[0], far_sem)
        put.start()
        put.wait()

    def half_first(place, spread, maps, over_maps, res, inverse, *refs):
        pieces, refs = refs[:RING], refs[RING:]
        first_out, inner, far, turned, buffer, sems, both, far_sem, tiles = refs
        out = both.at[:, : (own + over) * comps]
        copies = loads(inverse, 0, buffer, sems)
        for step, piece in enumerate(pieces):
            member = place[0, 2] + step
            member = jnp.where(member >= RING, member - RING, member)

            @pl.when(member * share < block)
            def _(piece=piece, member=member):
                tiles[:, pl.ds(pl.multiple_of(member * share, LANES), share)] = piece[...]

        everything = tiles[...]
        values = spread[...] + prolong_maps(everything, maps, at_own)
        both[:, (own + over) * comps :] = prolong_maps(everything, over_maps, 0)
        rf = jnp.zeros((rhs, own), F32)
        ff = jnp.zeros((rhs, own), F32)
        for k in range(comps):
            flipped = tile(values, k).T
            first_out[k] = flipped
            turned[:, k * LANES : (k + 1) * LANES] = flipped.astype(BF16)
            rf += res[k] * flipped
            ff += flipped * flipped
        inner[0:1, :] = jnp.sum(rf.T, axis=0, keepdims=True)
        inner[1:2, :] = jnp.sum(ff.T, axis=0, keepdims=True)
        product(copies, turned, buffer, None, out)
        put = pltpu.make_async_copy(both, far.at[0], far_sem)
        put.start()
        put.wait()

    def solve(got, part, maps, inverse, *refs):
        out, turned, buffer, sems, kept, kept_sems = refs
        size = out.shape[1]
        rest = kept.shape[1] - size
        if rest:
            bring_rest = pltpu.make_async_copy(part.at[0, :, pl.ds(size, rest)], kept.at[:, pl.ds(size, rest)], kept_sems.at[1])
            bring_rest.start()
        copies = loads(inverse, 1, buffer, sems)
        bring = pltpu.make_async_copy(part.at[0, :, pl.ds(0, size)], kept.at[:, pl.ds(0, size)], kept_sems.at[0])
        bring.start()
        arrived = dot(maps[at_take : at_take + over, :], got[:, :lanes])
        if rest:
            bring_rest.wait()
            arrived += kept[:, size:]
        for k in range(comps):
            turned[:, k * LANES : (k + 1) * LANES] = tile(arrived, k).T.astype(BF16)
        product(copies, turned, buffer, None, out)
        bring.wait()
        out[...] += kept[:, :size]

    def finish_first(got, total, parts, maps, send, res_own, over_maps, sol, token, own16, over16):
        token[...] = jnp.zeros((ROWS, LANES), F32)
        cams = own + over
        for k in range(comps):
            flipped = total[:, k * cams : (k + 1) * cams].T
            res_own[:, k * LANES : (k + 1) * LANES] = flipped[:own]
            flipped = flipped.astype(BF16)
            own16[:, k * LANES : (k + 1) * LANES] = flipped[:own]
            over16[:, k * LANES : (k + 1) * LANES] = flipped[own:]
        rows = maps[at_rows : at_rows + slots, :]
        take_t, own8 = rows[:, :over], rows[:, over : over + own]
        send[:, :lanes] = dot(take_t, over16[...]).astype(BF16)
        holder, kind = margin_places(got, take_t)
        cluster_maps(holder, kind, over_maps, 0)
        over8 = (iota((slots, over), 0) == holder * ROWS + kind).astype(F32).astype(BF16)
        pack(dot(own8, own16[...]) + dot(over8, over16[...]), None, send, lanes)
        _, tiles = group_total(parts)
        each_share = share // LANES
        for t in range(main):
            sol[:, t * LANES : (t + 1) * LANES] = tiles[t]
        member = iota((slots, LANES), 0) // ROWS % RING
        for j in range(each_share):
            value = jnp.zeros((slots, LANES), F32)
            for q in range(RING):
                if q * each_share + j < main:
                    value = jnp.where(member == q, repeat_rows(tiles[q * each_share + j], subs), value)
            at = lanes + block + j * LANES
            send[:, at : at + LANES] = value.astype(BF16)

    def margin_places(got, take_t):
        lane = iota((slots, LANES), 1)
        inner = iota((slots, LANES), 0) % ROWS
        ids = one_row(got[:, lanes + aux * LANES : lanes + (aux + 1) * LANES].astype(F32), cl_dev, subs)
        ids = jnp.sum(jnp.where(lane == inner, ids, 0.0), axis=1, keepdims=True)
        number = jnp.sum(take_t.astype(F32) * ids, axis=0, keepdims=True)
        holder = ((number + 0.5) * (1.0 / cl_dev)).astype(jnp.int32)
        return holder, number.astype(jnp.int32) - holder * cl_dev

    def cluster_maps(holder, kind, maps, base):
        rows = iota((slots, own), 0)
        hot = (rows == holder * ROWS + kind).astype(F32)
        maps[base : base + own, :] = hot.T.astype(BF16)
        for j in range(tail):
            hot_j = (rows == holder * ROWS + (cl_dev + j)).astype(F32)
            maps[base + (1 + j) * own : base + (2 + j) * own, :] = hot_j.T.astype(BF16)
        at = base + (1 + tail) * own
        maps[at : at + own, :] = jnp.broadcast_to(kind.astype(F32), (slots, own)).T.astype(BF16)

    def finish_second(total, parts, maps, send, res_own, over16):
        cams = own + over
        for k in range(comps):
            flipped = total[:, k * cams : (k + 1) * cams].T
            res_own[:, k * LANES : (k + 1) * LANES] = flipped[:own]
            over16[:, k * LANES : (k + 1) * LANES] = flipped[own:].astype(BF16)
        send[:, :lanes] = dot(maps[at_rows : at_rows + slots, :over], over16[...]).astype(BF16)
        summed, tiles = group_total(parts)
        each = main * ROWS
        inner = summed[each : each + 2] + summed[each + 2 : each + 4]
        low = inner - inner.astype(BF16).astype(F32)
        rest = low[0:1] - inner[0:1] / (inner[1:2] + EPSILON) * low[1:2]
        small = iota((ROWS, LANES), 0)
        for t in range(main):
            value = tiles[t]
            if t == aux:
                value = jnp.where(small == cl_dev, inner[0:1], value)
                value = jnp.where(small == cl_dev + 1, inner[1:2], value)
                value = jnp.where(small == cl_dev + 2, rest, value)
            send[:, lanes + t * LANES : lanes + (t + 1) * LANES] = repeat_rows(value, subs).astype(BF16)

    def prolong_maps(tiles, maps, base):
        kind = maps[base + (1 + tail) * own : base + (2 + tail) * own, :LANES].astype(F32)
        return prolong(tiles, maps[base : base + own, :], maps[base + own : base + (1 + tail) * own, :], kind)

    def combine(got, res_own, gives, members, sol, send, third, spread, token):
        token[...] = jnp.zeros((ROWS, LANES), F32)
        values = res_own[...] + dot(gives[:own, :], got[:, :lanes])
        spread[...] = values
        send[:, :lanes] = dot(gives[own:, :own], values.astype(BF16)).astype(BF16)
        total = jnp.sum(got[:, lanes : lanes + block].astype(F32).reshape(subs, ROWS, block), axis=0)
        for t in range(main):
            columns = slice(t * LANES, (t + 1) * LANES)
            value = tile(total, t) + members[:, columns] * sol[:, columns]
            send[:, lanes + t * LANES : lanes + (t + 1) * LANES] = repeat_rows(value, subs).astype(BF16)
        third[...] = got[:, lanes + block :]

    def end(got, res_own, first, gives, maps, out):
        applied = res_own[...] + dot(gives[...], got[:, :lanes])
        applied += prolong_maps(got[:, lanes:], maps, at_own)
        sums = got[:, lanes + aux * LANES :].astype(F32).reshape(subs, ROWS, LANES)
        sums = jnp.sum(sums, axis=0)
        scale = (sums[cl_dev : cl_dev + 1] + sums[cl_dev + 2 : cl_dev + 3]) / (sums[cl_dev + 1 : cl_dev + 2] + EPSILON)
        for k in range(comps):
            out[k] = first[k] - (scale * tile(applied, k)).T

    return dict(locals())


def place_of():
    index = lax.axis_index("group")
    return index % 2, index // 2


def pass_round(kept, given):
    turns = kept.shape[0]
    groups = 2 * turns
    other = lax.ppermute(given, "group", [(i, i ^ 1) for i in range(groups)])
    pieces = [kept[0], other[0]]
    for step in range(1, turns):
        piece = jnp.stack([kept[step], other[step]])
        pieces.append(lax.ppermute(piece, "group", [(i, (i - 2 * step) % groups) for i in range(groups)]))
    return pieces


def body(residual_in, local_inverse, coarse_inverse, cluster_of, margin_peer, margin_row):
    rhs, comps, own = residual_in.shape
    over = margin_row.shape[0]
    subs = lax.axis_size("sub")
    groups = lax.axis_size("group")
    cl_dev = coarse_inverse.shape[0] // comps
    width = local_inverse.shape[1]
    m = make(rhs, comps, own, over, subs, groups, cl_dev)
    slots, lanes, block, main, tail = m["slots"], m["lanes"], m["block"], m["main"], m["tail"]
    share = m["share"]
    each = main * ROWS
    inverse = local_inverse.reshape(comps, 2, own, width)
    residual = residual_in.transpose(1, 0, 2)
    cluster, peer, row = [values.reshape(1, -1) for values in (cluster_of, margin_peer, margin_row)]
    hbm = pl.BlockSpec(memory_space=pltpu.HBM)
    here = pl.BlockSpec(memory_space=pltpu.VMEM)
    vmem = pltpu.VMEM
    half_cost = dict(flops=rhs * width * width, moved=width * width)
    mark = ((ROWS, LANES), F32)
    spare = 16
    far = pl.BlockSpec(memory_space=pl.ANY)
    half_scratch = [
        vmem((rhs, lanes), BF16),
        vmem((comps, own, width), BF16),
        pltpu.SemaphoreType.DMA((comps,)),
    ]

    def swap(send):
        return exchange(send.reshape(subs, ROWS, send.shape[1]), "sub").reshape(send.shape)

    def coarse_parts(matrix, got, rows, inner, after=()):
        parts = kernel_call(
            functools.partial(m["coarse"], lanes, rows),
            [((groups, rows, LANES), BF16)],
            matrix,
            got,
            *inner,
            after=after,
        )[0]
        return exchange(parts, "group")

    def solve(got, part):
        return kernel_call(
            m["solve"],
            [((rhs, width), F32)],
            got,
            part,
            maps,
            inverse,
            in_specs=[here, far, here, hbm],
            scratch_shapes=half_scratch + [vmem(part.shape[1:], F32), pltpu.SemaphoreType.DMA((2,))],
            limit=48,
            **half_cost,
        )[0]

    with jax.named_scope("begin"):
        send, token = kernel_call(
            m["begin"],
            [((slots, block), BF16), mark],
            residual,
            cluster,
            peer,
            row,
            in_specs=[hbm] * 4,
            limit=60,
            scratch_shapes=[
                vmem((comps, rhs, own), F32),
                vmem((1, own), jnp.int32),
                vmem((1, over), jnp.int32),
                vmem((1, over), jnp.int32),
                vmem((own, lanes), BF16),
                pltpu.SemaphoreType.DMA((6,)),
            ],
        )
    with jax.named_scope("maps"):
        field16, maps = kernel_call(
            m["keep_maps"],
            [((own, lanes), BF16), ((m["map_rows"], slots), BF16)],
            residual,
            cluster,
            peer,
            after=[token],
        )
    with jax.named_scope("regroup"):
        member = lax.axis_index("sub") % RING
        place = jnp.stack(place_of() + (member,)).astype(jnp.int32).reshape(1, 3)
        columns = main * slots
        kept, given = kernel_call(
            m["prepare"],
            [((groups // 2, each, columns), BF16)] * 2,
            place,
            coarse_inverse,
            after=[token],
            in_specs=[pl.BlockSpec(memory_space=pltpu.SMEM), here],
            scratch_shapes=[vmem((groups, each, columns), BF16)],
            flops=2 * groups * each * columns * columns,
        )
    with jax.named_scope("answer"):
        got = swap(send)
        send, token = kernel_call(
            m["answer"], [((slots, lanes + block), BF16), mark], got, field16, cluster
        )
        gives, gives_late, members = kernel_call(
            m["keep_answer"],
            [((own + slots, slots), BF16), ((own, slots), BF16), ((ROWS, block), F32)],
            got,
            after=[token],
        )
    with jax.named_scope("own_half_first"):
        part, half_token = kernel_call(
            m["half"],
            [((spare, rhs, width), F32), mark],
            residual,
            inverse,
            after=[token],
            in_specs=[here, hbm],
            out_specs=[far, here],
            scratch_shapes=half_scratch + [vmem((rhs, width), F32), pltpu.SemaphoreType.DMA],
            **half_cost,
        )
    with jax.named_scope("regroup"):
        pieces = pass_round(kept, given)
        matrix, matrix_late = kernel_call(
            m["gather"],
            [((groups, each, columns), BF16)] * 2,
            place,
            *pieces,
            after=[half_token],
            in_specs=[pl.BlockSpec(memory_space=pltpu.SMEM)] + [here] * len(pieces),
        )
    got = swap(send)

    with jax.named_scope("coarse_first"):
        parts = coarse_parts(matrix, got, each, [], [half_token, members])
    with jax.named_scope("solve_first"):
        total = solve(got, part)
    with jax.named_scope("return_first"):
        send, res_own, over_maps, sol, token = kernel_call(
            m["finish_first"],
            [
                ((slots, lanes + block + share), BF16),
                ((own, lanes), F32),
                (((2 + tail) * own, slots), BF16),
                ((ROWS, block), F32),
                mark,
            ],
            got,
            total,
            parts,
            maps,
            scratch_shapes=[vmem((own, lanes), BF16), vmem((over, lanes), BF16)],
        )
        got = swap(send)
    with jax.named_scope("combine"):
        send, third, spread, token = kernel_call(
            m["combine"],
            [((slots, lanes + block), BF16), ((slots, share), BF16), ((own, lanes), F32), mark],
            got,
            res_own,
            gives,
            members,
            sol,
        )
    with jax.named_scope("own_half_second"):
        pieces_x = [third]
        for step in range(1, RING):
            turn = [(i, i // RING * RING + (i - step) % RING) for i in range(subs)]
            pieces_x.append(lax.ppermute(third, "sub", turn))
        first, inner, part = kernel_call(
            m["half_first"],
            [((comps, rhs, own), F32), ((2, LANES), F32), ((spare, rhs, width + lanes), F32)],

            place,
            spread,
            maps,
            over_maps,
            residual,
            inverse,
            *pieces_x,
            after=[token],
            in_specs=[pl.BlockSpec(memory_space=pltpu.SMEM)] + [here] * 4 + [hbm] + [here] * RING,
            out_specs=[here, here, far],
            scratch_shapes=half_scratch
            + [vmem((rhs, width + lanes), F32), pltpu.SemaphoreType.DMA, vmem((slots, block), BF16)],
            limit=48,
            **half_cost,
        )
    got = swap(send)
    with jax.named_scope("coarse_second"):
        parts = coarse_parts(matrix_late, got, each + 16, [inner])
    with jax.named_scope("solve_second"):
        total = solve(got, part)
    with jax.named_scope("return_second"):
        send, res_own = kernel_call(
            m["finish_second"],
            [((slots, lanes + block), BF16), ((own, lanes), F32)],
            total,
            parts,
            maps,
            scratch_shapes=[vmem((over, lanes), BF16)],
        )
        got = swap(send)
    with jax.named_scope("end"):
        second = kernel_call(m["end"], [((comps, rhs, own), F32)], got, res_own, first, gives_late, maps)[0]
    return first.transpose(1, 0, 2), second.transpose(1, 0, 2)


def solution(mesh):
    placed = (
        P(None, None, ("group", "sub")),
        P(("group", "sub"), None, None),
        P(("group", "sub"), None),
        P(("group", "sub")),
        P(("group", "sub"), None),
        P(("group", "sub")),
    )
    return jax.shard_map(
        body,
        mesh=mesh,
        in_specs=placed,
        out_specs=(P(None, None, ("group", "sub")), P(None, None, ("group", "sub"))),
        check_vma=False,
    )
```
